256 devices in a mesh: kz: 8 (over x, core), tile: 32 (over y, z).
Axes of the slice: x: 4, y: 4, z: 8, core: 2. Of those that a mesh axis runs over, the one named last changes fastest.
Arguments:
- coil_data: bfloat16 [8, 32, 8, 32, 2, 16, 128], P('kz', 'tile'), may hold values from -6 to 6
- frame_of: int32 [8, 32, 8, 32, 2], P('kz', 'tile'), may hold values from 0 to 999
- basis: bfloat16 [1000, 10], replicated, may hold values from -4 to 4
- sample_pos: float32 [8, 32, 8, 32, 2, 2, 128], P('kz', 'tile'), may hold values from 1.5 to 30.5, as said below
- window_at: int32 [8, 32, 8, 32, 2, 2], P('kz', 'tile'), may hold values from -2 to 639, as said below
- live_count: int32 [8, 32, 8, 32], P('kz', 'tile'), may hold values from 0 to 2, as said below
Outputs:
- image: bfloat16 [8, 640, 102400], P('kz', None, 'tile')
The draws below stay inside these ranges and needn't reach their ends.
Inputs may be any that keep to these rules, and one draw needn't show every extreme that they name: `live_count`: live slots of a pair are its first ones; destination tiles from 12 up to but not including 32 * 5 // 8 receive every slot from every acquiring device. `window_at`: the first entry (row0) lies in -2 to 18, the second (col0) in 0 to 639. `sample_pos`: the first entry lies in 1.5 to 2.5, the second in 1.5 to 32 - 1.5.
All inputs are finite; a program needn't handle non-finite values.
Results may differ from the reference program's by a relative error of at most 0.0077.
Values may be sent and summed in bfloat16 or wider, within the bound.
A program may use at most 192 MiB of HBM per device.

```python
import math
import jax
import jax.numpy as jnp
from jax import lax

PLANE = 640
RANK = 10
COILS = 8
FRAMES = 1000
BLOCK = 128
SLOTS = 2
WIN_ROWS = 4
WIN_COLS = 32
PARTITIONS = 8
TILES = 32
TILE_ROWS = 20


def draw_sample_pos(key, part):
    shape = (PARTITIONS, TILES, PARTITIONS, TILES, SLOTS, BLOCK)
    key_row, key_col = jax.random.split(key)
    rows = jax.random.uniform(key_row, shape, jnp.float32, 1.5, 2.5)
    cols = jax.random.uniform(key_col, shape, jnp.float32, 1.5, WIN_COLS - 1.5)
    return jnp.stack([rows, cols], axis=5)


def draw_window_at(key, part):
    shape = (PARTITIONS, TILES, PARTITIONS, TILES, SLOTS)
    key_row, key_col = jax.random.split(jax.random.fold_in(key, 7))
    rows = jax.random.randint(key_row, shape, -2, TILE_ROWS - 1)
    cols = jax.random.randint(key_col, shape, 0, PLANE)
    return jnp.stack([rows, cols], axis=5).astype(jnp.int32)


def draw_live_count(key, part):
    shape = (PARTITIONS, TILES, PARTITIONS, TILES)
    base = jax.random.randint(jax.random.fold_in(key, 11), shape, 0, SLOTS + 1)
    tile_idx = jnp.arange(TILES, dtype=jnp.int32)[None, :, None, None]
    hot = (tile_idx >= TILES * 3 // 8) & (tile_idx < TILES * 5 // 8)
    return jnp.where(hot, SLOTS, base).astype(jnp.int32)


def place_ends(values, stream_key, smallest, largest):
    spot = [jax.random.randint(jax.random.fold_in(stream_key, axis), (), 0, length) for axis, length in enumerate(values.shape)]
    widest = values.shape.index(max(values.shape))
    next_to = spot[:widest] + [(spot[widest] + 1) % values.shape[widest]] + spot[widest + 1:]
    return values.at[tuple(spot)].set(smallest).at[tuple(next_to)].set(largest)


def shard_levels(own_key, extent, cuts, smallest, largest):
    factor_of = 1.0
    for position, blocks in cuts:
        steps = jax.random.uniform(jax.random.fold_in(jax.random.fold_in(own_key, 6), position), (blocks,), jnp.float32, smallest / len(cuts), largest / len(cuts))
        factor_of = factor_of * jnp.repeat(jnp.exp(steps), extent[position] // blocks).reshape((-1,) + (1,) * (len(extent) - 1 - position))
    return factor_of


def noise(stream_key, shape, scale, limit, shards=(), held_as=jnp.bfloat16):
    gain = shard_levels(stream_key, shape, shards, -0.22, 0.18) if shards else 1.0
    drawn = jax.random.normal(stream_key, shape, jnp.float32) * scale * gain
    return jnp.minimum(jnp.maximum(drawn, -limit), limit).astype(held_as)


def setup_inputs(seed: int = 0) -> dict:
    key_of = jax.random.split(jax.random.key(seed), 7)
    coil_data = noise(key_of[0], (PARTITIONS, TILES, PARTITIONS, TILES, SLOTS, 2 * COILS, BLOCK), 1.0, 6.0, ((0, 8), (1, 32)))
    frame_of = place_ends(jax.random.randint(key_of[1], (PARTITIONS, TILES, PARTITIONS, TILES, SLOTS), 0, FRAMES), jax.random.fold_in(key_of[1], 1), 0, FRAMES - 1).astype(jnp.int32)
    basis = noise(key_of[2], (FRAMES, RANK), 1.0, 4.0)
    sample_pos = draw_sample_pos(jax.random.fold_in(key_of[6], 71), 0)
    window_at = draw_window_at(jax.random.fold_in(key_of[6], 71), 0)
    live_count = draw_live_count(jax.random.fold_in(key_of[6], 71), 0)
    return {"coil_data": coil_data, "frame_of": frame_of, "basis": basis, "sample_pos": sample_pos, "window_at": window_at, "live_count": live_count}


def taper(dist):
    inner = 1.0 - (dist / 1.5) ** 2
    return jnp.maximum(inner, 0.0) ** 2


def project(blocks, coeffs):
    count = blocks.shape[0]
    coils = blocks.shape[1] // 2
    ranks = coeffs.shape[1]
    samples = blocks.shape[2]
    data = blocks.astype(jnp.float32).reshape(count, 2, 1, coils, samples)
    scale = coeffs.astype(jnp.float32).reshape(count, 1, ranks, 1, 1)
    return (data * scale).reshape(count, 2 * ranks * coils, samples).astype(jnp.bfloat16)


def wide_product(weights, values):
    return jnp.einsum("gwb,gcb->gwc", weights.astype(jnp.float32), values.astype(jnp.float32))


def grid_tile(proj, offsets, corners, alive, tile_rows, plane):
    count, width, samples = proj.shape
    group = 64
    row_cells = jnp.arange(WIN_ROWS, dtype=jnp.float32)
    col_cells = jnp.arange(WIN_COLS, dtype=jnp.float32)
    cells = jnp.arange(WIN_ROWS * WIN_COLS, dtype=jnp.int32)
    cell_row = cells // WIN_COLS
    cell_col = cells % WIN_COLS

    def step(acc, items):
        values, place, corner, living = items
        row_k = taper(row_cells[None, :, None] - place[:, 0:1, :])
        col_k = taper(col_cells[None, :, None] - place[:, 1:2, :])
        weights = (row_k[:, :, None, :] * col_k[:, None, :, :]).reshape(group, WIN_ROWS * WIN_COLS, samples)
        weights = (weights * living[:, None, None]).astype(jnp.bfloat16)
        contrib = wide_product(weights, values)
        rows = corner[:, 0:1] + 2 + cell_row[None, :]
        cols = (corner[:, 1:2] + cell_col[None, :]) % plane
        acc = acc.at[rows.reshape(-1), cols.reshape(-1)].add(contrib.reshape(-1, width))
        return acc, None

    start = jnp.zeros((tile_rows + 4, plane, width), jnp.float32)
    items = (proj.reshape(-1, group, width, samples), offsets.reshape(-1, group, 2, samples),
             corners.reshape(-1, group, 2), alive.reshape(-1, group))
    acc, _ = lax.scan(step, start, items)
    return acc


def tables(n):
    idx = jnp.arange(n, dtype=jnp.int32)
    phase = ((idx[:, None] * idx[None, :]) % n).astype(jnp.float32) * (2.0 * math.pi / n)
    return jnp.cos(phase).astype(jnp.bfloat16), jnp.sin(phase).astype(jnp.bfloat16)


def combine(first, second, half):
    return jnp.concatenate([first[..., :half] - second[..., half:], second[..., :half] + first[..., half:]], axis=-1)


def reference(coil_data, frame_of, basis, sample_pos, window_at, live_count):
    parts = coil_data.shape[0]
    tiles = coil_data.shape[1]
    slots = coil_data.shape[4]
    pair = coil_data.shape[5]
    samples = coil_data.shape[6]
    width = 2 * basis.shape[1] * (pair // 2)
    half = width // 2
    tile_rows = PLANE // tiles
    cos_tab, sin_tab = tables(PLANE)
    slot_idx = jnp.arange(slots, dtype=jnp.int32)

    def one_part(a):
        data_a = lax.dynamic_index_in_dim(coil_data, a, 2, False)
        frames_a = lax.dynamic_index_in_dim(frame_of, a, 2, False)
        pos_a = lax.dynamic_index_in_dim(sample_pos, a, 0, False)
        win_a = lax.dynamic_index_in_dim(window_at, a, 0, False)
        live_a = lax.dynamic_index_in_dim(live_count, a, 0, False)

        def one_tile(total, t):
            blocks = lax.dynamic_index_in_dim(data_a, t, 2, False)
            frames = lax.dynamic_index_in_dim(frames_a, t, 2, False)
            offsets = lax.dynamic_index_in_dim(pos_a, t, 0, False)
            corners = lax.dynamic_index_in_dim(win_a, t, 0, False)
            counts = lax.dynamic_index_in_dim(live_a, t, 0, False)
            proj = project(blocks.reshape(-1, pair, samples), basis[frames.reshape(-1)])
            alive = (slot_idx[None, None, :] < counts[:, :, None]).astype(jnp.float32)
            acc = grid_tile(proj, offsets.reshape(-1, 2, samples), corners.reshape(-1, 2), alive.reshape(-1), tile_rows, PLANE)
            rows = (t * tile_rows - 2 + jnp.arange(tile_rows + 4, dtype=jnp.int32)) % PLANE
            return total.at[rows].add(acc), None

        total, _ = lax.scan(one_tile, jnp.zeros((PLANE, PLANE, width), jnp.float32), jnp.arange(tiles, dtype=jnp.int32))
        grid = total.astype(jnp.bfloat16).astype(jnp.float32)
        first = jnp.einsum("xkq,ky->xyq", grid, cos_tab.astype(jnp.float32))
        second = jnp.einsum("xkq,ky->xyq", grid, sin_tab.astype(jnp.float32))
        mid = combine(first, second, half).astype(jnp.bfloat16).astype(jnp.float32)
        first = jnp.einsum("kyq,kx->xyq", mid, cos_tab.astype(jnp.float32))
        second = jnp.einsum("kyq,kx->xyq", mid, sin_tab.astype(jnp.float32))
        result = (combine(first, second, half) * (1.0 / PLANE)).astype(jnp.bfloat16)
        return result.reshape(PLANE, PLANE * width)

    return lax.map(one_part, jnp.arange(parts, dtype=jnp.int32))
```

```python
import functools
import math

import jax
import jax.numpy as jnp
from jax import lax
from jax.experimental import pallas as pl
from jax.experimental.pallas import tpu as pltpu
from jax.sharding import PartitionSpec as P

PLANE = 640
WIN_ROWS = 4
WIN_COLS = 32
TILE_ROWS = 20
WIDE = 40
PAD = 680
LANES = 128
HALF = 80
MB = 1024 * 1024


def taper(dist):
    inner = 1.0 - (dist * (1.0 / 1.5)) * (dist * (1.0 / 1.5))
    inner = jnp.maximum(inner, 0.0)
    return inner * inner


def grid_slots(row_ref, col_ref, live_ref, coef_ref, pos_ref, data_ref, acc_ref, batch):
    count = data_ref.shape[0]
    row_cell = lax.broadcasted_iota(jnp.int32, (8, LANES), 0)
    col_cell = lax.broadcasted_iota(jnp.int32, (WIDE, LANES), 0)
    zero = jnp.zeros((LANES - HALF, LANES), jnp.bfloat16)

    def contribution(s):
        col0 = col_ref[s]
        shift = jnp.bitwise_and(col0, 7)
        place = pos_ref[s]
        u = place[0:1, :]
        v = place[1:2, :]
        row_k = taper(row_cell.astype(jnp.float32) - u) * live_ref[s]
        col_k = taper((col_cell - shift).astype(jnp.float32) - v)
        weight = jnp.concatenate([row_k[i : i + 1, :] * col_k for i in range(WIN_ROWS)], axis=0)
        weight = weight.astype(jnp.bfloat16)
        data = data_ref[s].astype(jnp.float32)
        re, im = data[0:8], data[8:16]
        scale = [coef_ref[s * 10 + r] for r in range(10)]
        re = jnp.concatenate([re * c for c in scale], axis=0).astype(jnp.bfloat16)
        im = jnp.concatenate([im * c for c in scale], axis=0).astype(jnp.bfloat16)
        values = jnp.concatenate([re, zero, im, zero], axis=0)
        return lax.dot_general(
            weight, values, (((1,), (1,)), ((), ())), preferred_element_type=jnp.float32
        )

    def step(b, carry):
        slots = [b * batch + k for k in range(batch)]
        parts = [contribution(s) for s in slots]
        for s, part in zip(slots, parts):
            row = row_ref[s] + 2
            start = pl.multiple_of(jnp.bitwise_and(col_ref[s], -8), 8)
            for i in range(WIN_ROWS):
                at = (row + i, pl.ds(start, WIDE), slice(None))
                acc_ref[at] += part[i * WIDE : (i + 1) * WIDE]
        return carry

    lax.fori_loop(0, count // batch, step, 0)


def first_grid(row_ref, col_ref, live_ref, coef_ref, pos_ref, data_ref, acc_ref, *, batch):
    def clear(k, carry):
        acc_ref[k] = jnp.zeros(acc_ref.shape[1:], jnp.float32)
        return carry

    lax.fori_loop(0, acc_ref.shape[0], clear, 0)
    grid_slots(row_ref, col_ref, live_ref, coef_ref, pos_ref, data_ref, acc_ref, batch)


def second_grid(row_ref, col_ref, live_ref, coef_ref, pos_ref, data_ref, before_ref,
                inner_ref, own_ref, up_ref, down_ref, acc_ref, sem, *, batch):
    copy = pltpu.make_async_copy(before_ref, acc_ref, sem)
    copy.start()
    copy.wait()
    grid_slots(row_ref, col_ref, live_ref, coef_ref, pos_ref, data_ref, acc_ref, batch)

    def row_of(k):
        wrap = acc_ref[k, 0:WIDE, :] + acc_ref[k, PLANE:PAD, :]
        return jnp.concatenate([wrap, acc_ref[k, WIDE:PLANE, :]], axis=0)

    for k in range(2):
        up_ref[k] = row_of(k).astype(jnp.bfloat16)
        down_ref[k] = row_of(TILE_ROWS + 2 + k).astype(jnp.bfloat16)
        own_ref[k] = row_of(2 + k)
        own_ref[2 + k] = row_of(TILE_ROWS + k)

    def emit(k, carry):
        inner_ref[k] = row_of(k + 4).astype(jnp.bfloat16)
        return carry

    lax.fori_loop(0, TILE_ROWS - 4, emit, 0)


SMEM = pl.BlockSpec(memory_space=pltpu.SMEM)
VMEM = pl.BlockSpec(memory_space=pltpu.VMEM)
ANY = pl.BlockSpec(memory_space=pl.ANY)


def grid_first(rows, cols, live, coef, pos, data, batch=4):
    return pl.pallas_call(
        functools.partial(first_grid, batch=batch),
        out_shape=jax.ShapeDtypeStruct((TILE_ROWS + 4, PAD, 2 * LANES), jnp.float32),
        in_specs=[SMEM] * 4 + [VMEM] * 2,
        out_specs=VMEM,
        compiler_params=pltpu.CompilerParams(vmem_limit_bytes=32 * MB),
        cost_estimate=pl.CostEstimate(flops=3 * 10**9, bytes_accessed=20 * MB, transcendentals=0),
        name="grid_first",
    )(rows, cols, live, coef, pos, data)


def grid_second(rows, cols, live, coef, pos, data, before, batch=4):
    wide = 2 * LANES
    return pl.pallas_call(
        functools.partial(second_grid, batch=batch),
        out_shape=[
            jax.ShapeDtypeStruct((TILE_ROWS - 4, PLANE, wide), jnp.bfloat16),
            jax.ShapeDtypeStruct((4, PLANE, wide), jnp.float32),
            jax.ShapeDtypeStruct((2, PLANE, wide), jnp.bfloat16),
            jax.ShapeDtypeStruct((2, PLANE, wide), jnp.bfloat16),
        ],
        in_specs=[SMEM] * 4 + [VMEM] * 2 + [ANY],
        out_specs=[VMEM] * 4,
        scratch_shapes=[
            pltpu.VMEM((TILE_ROWS + 4, PAD, wide), jnp.float32),
            pltpu.SemaphoreType.DMA,
        ],
        compiler_params=pltpu.CompilerParams(vmem_limit_bytes=40 * MB),
        cost_estimate=pl.CostEstimate(flops=3 * 10**9, bytes_accessed=20 * MB, transcendentals=0),
        name="grid_second",
    )(rows, cols, live, coef, pos, data, before)


def interleave(pieces):
    lane = lax.broadcasted_iota(jnp.int32, pieces[0].shape, 1)
    p = [pieces[0]] + [pltpu.roll(pieces[k], (HALF * k) % LANES, 1) for k in range(1, 8)]
    return [
        jnp.where(lane < 80, p[0], p[1]),
        jnp.where(lane < 32, p[1], jnp.where(lane < 112, p[2], p[3])),
        jnp.where(lane < 64, p[3], p[4]),
        jnp.where(lane < 16, p[4], jnp.where(lane < 96, p[5], p[6])),
        jnp.where(lane < 48, p[6], p[7]),
    ]


def ky_rows(table_ref, plane_of, count, re_ref, im_ref):
    def transform(k, carry):
        plane = plane_of(k)
        re, im = plane[:, :LANES], plane[:, LANES:]
        stacked = jnp.concatenate(
            [plane, jnp.concatenate([-im, re], axis=1)], axis=0
        )
        out = jnp.dot(table_ref[...], stacked, preferred_element_type=jnp.float32)
        at = pl.ds(pl.multiple_of(k * PLANE, PLANE), PLANE)
        re_ref[at, :] = out[:, :LANES]
        im_ref[at, :] = out[:, LANES:]
        return carry

    lax.fori_loop(0, count, transform, 0)


def ky_inner(table_ref, grid_ref, out_ref, re_ref, im_ref):
    ky_rows(table_ref, lambda k: grid_ref[k], TILE_ROWS - 4, re_ref, im_ref)

    def block(d, carry):
        for b in range(5):
            halves = []
            for g in range(2):
                pieces = []
                for j in range(4):
                    at = pl.ds(g * 8 * PLANE + d * 20 + b * 4 + j, 8, stride=PLANE)
                    pieces += [re_ref[at, :], im_ref[at, :]]
                halves.append(jnp.concatenate(interleave(pieces), axis=1))
            out_ref[d, :, b * PLANE : (b + 1) * PLANE] = jnp.concatenate(halves, axis=0).astype(jnp.bfloat16)
        return carry

    lax.fori_loop(0, 32, block, 0)


def ky_edge(table_ref, own_ref, above_ref, below_ref, out_ref, grid_ref, re_ref, im_ref):
    for k in range(2):
        grid_ref[k] = (own_ref[k] + above_ref[k].astype(jnp.float32)).astype(jnp.bfloat16)
        grid_ref[2 + k] = (own_ref[2 + k] + below_ref[k].astype(jnp.float32)).astype(jnp.bfloat16)
    ky_rows(table_ref, lambda k: grid_ref[k], 4, re_ref, im_ref)

    def block(d, carry):
        for b in range(5):
            pieces = []
            for j in range(4):
                at = pl.ds(d * 20 + b * 4 + j, 4, stride=PLANE)
                pieces += [re_ref[at, :], im_ref[at, :]]
            out = jnp.concatenate(interleave(pieces), axis=1)
            out_ref[d, :, b * PLANE : (b + 1) * PLANE] = out.astype(jnp.bfloat16)
        return carry

    lax.fori_loop(0, 32, block, 0)


def transform_inner(table, grid):
    rows = TILE_ROWS - 4
    return pl.pallas_call(
        ky_inner,
        out_shape=jax.ShapeDtypeStruct((32, rows, 5 * PLANE), jnp.bfloat16),
        in_specs=[VMEM] * 2,
        out_specs=VMEM,
        scratch_shapes=[pltpu.VMEM((rows * PLANE, LANES), jnp.float32)] * 2,
        compiler_params=pltpu.CompilerParams(vmem_limit_bytes=40 * MB),
        cost_estimate=pl.CostEstimate(flops=8 * 10**9, bytes_accessed=10 * MB, transcendentals=0),
        name="ky_inner",
    )(table, grid)


def transform_edge(table, own, above, below):
    return pl.pallas_call(
        ky_edge,
        out_shape=jax.ShapeDtypeStruct((32, 4, 5 * PLANE), jnp.bfloat16),
        in_specs=[VMEM] * 4,
        out_specs=VMEM,
        scratch_shapes=[
            pltpu.VMEM((4, PLANE, 2 * LANES), jnp.bfloat16),
            pltpu.VMEM((4 * PLANE, LANES), jnp.float32),
            pltpu.VMEM((4 * PLANE, LANES), jnp.float32),
        ],
        compiler_params=pltpu.CompilerParams(vmem_limit_bytes=32 * MB),
        cost_estimate=pl.CostEstimate(flops=2 * 10**9, bytes_accessed=4 * MB, transcendentals=0),
        name="ky_edge",
    )(table, own, above, below)


def kx_block(inner_table_ref, edge_table_ref, inner_ref, edge_ref, out_ref):
    lane = lax.rem(lax.broadcasted_iota(jnp.int32, (320, PLANE), 1), 2 * HALF)
    real = lane < HALF
    for h in range(2):
        rows = slice(320 * h, 320 * (h + 1))

        def product(part):
            return jnp.dot(
                inner_table_ref[part, rows, :], inner_ref[...], preferred_element_type=jnp.float32
            ) + jnp.dot(edge_table_ref[part, rows, :], edge_ref[...], preferred_element_type=jnp.float32)

        first = product(0)
        second = product(1)
        ahead = pltpu.roll(second, PLANE - HALF, 1)
        behind = pltpu.roll(second, HALF, 1)
        out = first + jnp.where(real, -ahead, behind)
        out_ref[rows, :] = (out * (1.0 / PLANE)).astype(jnp.bfloat16)


def transform_kx(inner_table, edge_table, inner, edge):
    columns = inner.shape[1]
    return pl.pallas_call(
        kx_block,
        grid=(columns // PLANE,),
        out_shape=jax.ShapeDtypeStruct((PLANE, columns), jnp.bfloat16),
        in_specs=[
            VMEM,
            VMEM,
            pl.BlockSpec((512, PLANE), lambda n: (0, n)),
            pl.BlockSpec((128, PLANE), lambda n: (0, n)),
        ],
        out_specs=pl.BlockSpec((PLANE, PLANE), lambda n: (0, n)),
        compiler_params=pltpu.CompilerParams(vmem_limit_bytes=40 * MB),
        cost_estimate=pl.CostEstimate(flops=8 * 10**9, bytes_accessed=10 * MB, transcendentals=0),
        name="kx",
    )(inner_table, edge_table, inner, edge)


def tables(n):
    idx = jnp.arange(n, dtype=jnp.int32)
    phase = (idx[:, None] * idx[None, :] % n).astype(jnp.float32) * (2.0 * math.pi / n)
    return (jnp.cos(phase).astype(jnp.bfloat16), jnp.sin(phase).astype(jnp.bfloat16))


def make_tables():
    cos_tab, sin_tab = tables(PLANE)
    ky_table = jnp.concatenate([cos_tab, sin_tab], axis=1)
    both = jnp.stack([cos_tab, sin_tab]).reshape(2, PLANE, 32, TILE_ROWS)
    inner_table = both[..., 2:18].reshape(2, PLANE, 512)
    edge_table = jnp.concatenate([both[..., 0:2], both[..., 18:20]], axis=-1).reshape(2, PLANE, 128)
    return ky_table, inner_table, edge_table


def neighbour(value, steps):
    count = lax.axis_size("tile")
    pairs = [(source, (source + steps) % count) for source in range(count)]
    return lax.ppermute(value, "tile", pairs)


def body(coil_data, frame_of, basis, sample_pos, window_at, live_count):
    axes = ("kz", "tile")
    devices = 256
    data = coil_data.reshape(devices, 2, 16, LANES)
    arrived = [
        lax.all_to_all(data[:, s], axes, split_axis=0, concat_axis=0, tiled=True) for s in range(2)
    ]
    me = lax.axis_index("kz") * lax.axis_size("tile") + lax.axis_index("tile")
    gathered = lax.all_gather(frame_of.reshape(4, LANES), axes, axis=0, tiled=False)
    frames = lax.dynamic_slice(gathered.reshape(devices, devices, 2), (0, me, 0), (devices, 1, 2))
    frames = frames.reshape(devices, 2)
    coef = basis[frames.T.reshape(-1)].astype(jnp.float32).reshape(2, devices * 10)
    window = window_at.reshape(devices, 2, 2)
    live = (jnp.arange(2)[:, None] < live_count.reshape(1, devices)).astype(jnp.float32)
    pos = sample_pos.reshape(devices, 2, 2, LANES)

    def slot(s):
        return window[:, s, 0], window[:, s, 1], live[s], coef[s], pos[:, s], arrived[s]

    ky_table, inner_table, edge_table = make_tables()
    before = grid_first(*slot(0))
    inner, own, up, down = grid_second(*slot(1), before)
    from_above = neighbour(down, 1)
    from_below = neighbour(up, -1)
    mid_inner = transform_inner(ky_table, inner)
    mid_inner = lax.all_to_all(mid_inner, "tile", split_axis=0, concat_axis=0, tiled=True)
    mid_edge = transform_edge(ky_table, own, from_above, from_below)
    mid_edge = lax.all_to_all(mid_edge, "tile", split_axis=0, concat_axis=0, tiled=True)
    image = transform_kx(
        inner_table, edge_table, mid_inner.reshape(512, 5 * PLANE), mid_edge.reshape(128, 5 * PLANE)
    )
    return image[None]


def solution(mesh):
    return jax.shard_map(
        body,
        mesh=mesh,
        in_specs=(
            P("kz", "tile", None, None, None, None, None),
            P("kz", "tile", None, None, None),
            P(),
            P("kz", "tile", None, None, None, None, None),
            P("kz", "tile", None, None, None, None),
            P("kz", "tile", None, None),
        ),
        out_specs=P("kz", None, "tile"),
        check_vma=False,
    )
```

```python
import functools
import math

import jax
import jax.numpy as jnp
from jax import lax
from jax.experimental import pallas as pl
from jax.experimental.pallas import tpu as pltpu
from jax.sharding import PartitionSpec as P
import ml_dtypes
import numpy as np

PLANE = 640
WIN_ROWS = 4
WIN_COLS = 32
TILE_ROWS = 20
WIDE = 40
PAD = 680
LANES = 128
HALF = 80
MB = 1024 * 1024


def taper(dist):
    inner = 1.0 - (dist * (1.0 / 1.5)) * (dist * (1.0 / 1.5))
    inner = jnp.maximum(inner, 0.0)
    return inner * inner


def grid_slots(row_ref, col_ref, live_ref, coef_ref, pos_ref, data_ref, acc_ref, batch):
    count = data_ref.shape[0]
    row_cell = lax.broadcasted_iota(jnp.int32, (8, LANES), 0)
    col_cell = lax.broadcasted_iota(jnp.int32, (WIDE, LANES), 0)
    zero = jnp.zeros((LANES - HALF, LANES), jnp.bfloat16)

    def contribution(s):
        col0 = col_ref[s]
        shift = jnp.bitwise_and(col0, 7)
        place = pos_ref[s]
        u = place[0:1, :]
        v = place[1:2, :]
        row_k = taper(row_cell.astype(jnp.float32) - u) * live_ref[s]
        col_k = taper((col_cell - shift).astype(jnp.float32) - v)
        weight = jnp.concatenate([row_k[i : i + 1, :] * col_k for i in range(WIN_ROWS)], axis=0)
        weight = weight.astype(jnp.bfloat16)
        data = data_ref[s].astype(jnp.float32)
        re, im = data[0:8], data[8:16]
        scale = [coef_ref[s * 10 + r] for r in range(10)]
        re = jnp.concatenate([re * c for c in scale], axis=0).astype(jnp.bfloat16)
        im = jnp.concatenate([im * c for c in scale], axis=0).astype(jnp.bfloat16)
        values = jnp.concatenate([re, zero, im, zero], axis=0)
        return lax.dot_general(
            weight, values, (((1,), (1,)), ((), ())), preferred_element_type=jnp.float32
        )

    def step(b, carry):
        slots = [b * batch + k for k in range(batch)]
        parts = [contribution(s) for s in slots]
        for s, part in zip(slots, parts):
            row = row_ref[s] + 2
            start = pl.multiple_of(jnp.bitwise_and(col_ref[s], -8), 8)
            for i in range(WIN_ROWS):
                at = (row + i, pl.ds(start, WIDE), slice(None))
                acc_ref[at] += part[i * WIDE : (i + 1) * WIDE]
        return carry

    lax.fori_loop(0, count // batch, step, 0)


def grid_kernel(row_ref, col_ref, live_ref, coef_ref, pos_ref, data_ref,
                inner_ref, own_ref, up_ref, down_ref, acc_ref, *, batch):
    def clear(k, carry):
        acc_ref[k] = jnp.zeros(acc_ref.shape[1:], jnp.float32)
        return carry

    lax.fori_loop(0, acc_ref.shape[0], clear, 0)
    grid_slots(row_ref, col_ref, live_ref, coef_ref, pos_ref, data_ref, acc_ref, batch)

    def row_of(k):
        wrap = acc_ref[k, 0:WIDE, :] + acc_ref[k, PLANE:PAD, :]
        return jnp.concatenate([wrap, acc_ref[k, WIDE:PLANE, :]], axis=0)

    for k in range(2):
        up_ref[k] = row_of(k).astype(jnp.bfloat16)
        down_ref[k] = row_of(TILE_ROWS + 2 + k).astype(jnp.bfloat16)
        own_ref[k] = row_of(2 + k)
        own_ref[2 + k] = row_of(TILE_ROWS + k)

    def emit(k, carry):
        inner_ref[k] = row_of(k + 4).astype(jnp.bfloat16)
        return carry

    lax.fori_loop(0, TILE_ROWS - 4, emit, 0)


SMEM = pl.BlockSpec(memory_space=pltpu.SMEM)
VMEM = pl.BlockSpec(memory_space=pltpu.VMEM)


def grid_tile(rows, cols, live, coef, pos, data, batch=4):
    wide = 2 * LANES
    return pl.pallas_call(
        functools.partial(grid_kernel, batch=batch),
        out_shape=[
            jax.ShapeDtypeStruct((TILE_ROWS - 4, PLANE, wide), jnp.bfloat16),
            jax.ShapeDtypeStruct((4, PLANE, wide), jnp.float32),
            jax.ShapeDtypeStruct((2, PLANE, wide), jnp.bfloat16),
            jax.ShapeDtypeStruct((2, PLANE, wide), jnp.bfloat16),
        ],
        in_specs=[SMEM] * 4 + [VMEM] * 2,
        out_specs=[VMEM] * 4,
        scratch_shapes=[pltpu.VMEM((TILE_ROWS + 4, PAD, wide), jnp.float32)],
        compiler_params=pltpu.CompilerParams(vmem_limit_bytes=40 * MB),
        cost_estimate=pl.CostEstimate(flops=6 * 10**9, bytes_accessed=20 * MB, transcendentals=0),
        name="grid_tile",
    )(rows, cols, live, coef, pos, data)


def interleave(pieces):
    lane = lax.broadcasted_iota(jnp.int32, pieces[0].shape, 1)
    p = [pieces[0]] + [pltpu.roll(pieces[k], (HALF * k) % LANES, 1) for k in range(1, 8)]
    return [
        jnp.where(lane < 80, p[0], p[1]),
        jnp.where(lane < 32, p[1], jnp.where(lane < 112, p[2], p[3])),
        jnp.where(lane < 64, p[3], p[4]),
        jnp.where(lane < 16, p[4], jnp.where(lane < 96, p[5], p[6])),
        jnp.where(lane < 48, p[6], p[7]),
    ]


def mid_kernel(ky_ref, inner_table_ref, edge_table_ref, grid_ref, own_ref, up_ref, down_ref, out_ref,
               send_in, send_ed, recv_in, recv_ed, halo, rot, edge_grid, edge_rot, re_ref, im_ref, edge_kx,
               halo_send, halo_recv, send_sem_in, recv_sem_in, send_sem_ed, recv_sem_ed):
    count = lax.axis_size("tile")
    me = lax.axis_index("tile")
    above = lax.rem(me + count - 1, count)
    below = lax.rem(me + 1, count)
    stages = ky_ref.shape[0]
    inner_rows = TILE_ROWS - 4

    barrier = pltpu.get_barrier_semaphore()

    def greet(k, carry):
        pl.semaphore_signal(
            barrier, inc=1, device_id={"tile": lax.rem(me + k, count)}, device_id_type=pl.DeviceIdType.MESH
        )
        return carry

    lax.fori_loop(1, count, greet, 0)
    pl.semaphore_wait(barrier, count - 1)

    def halo_copy(source, way, peer):
        return pltpu.make_async_remote_copy(
            src_ref=source, dst_ref=halo.at[way], send_sem=halo_send.at[way], recv_sem=halo_recv.at[way],
            device_id={"tile": peer}, device_id_type=pl.DeviceIdType.MESH,
        )

    to_below = halo_copy(down_ref, 0, below)
    to_above = halo_copy(up_ref, 1, above)
    to_below.start()
    to_above.start()

    def turned(plane):
        return jnp.concatenate([-plane[:, LANES:], plane[:, :LANES]], axis=1)

    def turn(k, carry):
        rot[k] = turned(grid_ref[k])
        return carry

    lax.fori_loop(0, inner_rows, turn, 0)

    def rows_of(b, k, plane_ref, turned_ref):
        out = jnp.dot(ky_ref[b, :, :PLANE], plane_ref[k], preferred_element_type=jnp.float32)
        out += jnp.dot(ky_ref[b, :, PLANE:], turned_ref[k], preferred_element_type=jnp.float32)
        at = pl.ds(pl.multiple_of(k * LANES, LANES), LANES)
        re_ref[at, :] = out[:, :LANES]
        im_ref[at, :] = out[:, LANES:]

    def pieces_of(start, size):
        pieces = []
        for j in range(4):
            at = pl.ds(start + j, size, stride=LANES)
            pieces += [re_ref[at, :], im_ref[at, :]]
        return jnp.concatenate(interleave(pieces), axis=1)

    def send_all(b, send, recv, send_sem, recv_sem):
        recv[b, me] = send[b, me]

        def to_peer(k, carry):
            peer = lax.rem(me + k, count)
            pltpu.make_async_remote_copy(
                src_ref=send.at[b, peer], dst_ref=recv.at[b, me],
                send_sem=send_sem.at[b], recv_sem=recv_sem.at[b],
                device_id={"tile": peer}, device_id_type=pl.DeviceIdType.MESH,
            ).start()
            return carry

        lax.fori_loop(1, count, to_peer, 0)

    def stage(b, carry):
        def inner_row(k, carry):
            rows_of(b, k, grid_ref, rot)
            return carry

        lax.fori_loop(0, inner_rows, inner_row, 0)

        def inner_pack(d, carry):
            halves = [pieces_of(g * 8 * LANES + d * 4, 8) for g in range(2)]
            send_in[b, d] = jnp.concatenate(halves, axis=0).astype(jnp.bfloat16)
            return carry

        lax.fori_loop(0, count, inner_pack, 0)
        send_all(b, send_in, recv_in, send_sem_in, recv_sem_in)

        @pl.when(b == 0)
        def _():
            to_below.wait()
            to_above.wait()
            for k in range(2):
                edge_grid[k] = (own_ref[k] + halo[0, k].astype(jnp.float32)).astype(jnp.bfloat16)
                edge_grid[2 + k] = (own_ref[2 + k] + halo[1, k].astype(jnp.float32)).astype(jnp.bfloat16)
            for k in range(4):
                edge_rot[k] = turned(edge_grid[k])

        def edge_row(k, carry):
            rows_of(b, k, edge_grid, edge_rot)
            return carry

        lax.fori_loop(0, 4, edge_row, 0)

        def edge_pack(d, carry):
            send_ed[b, d] = pieces_of(d * 4, 4).astype(jnp.bfloat16)
            return carry

        lax.fori_loop(0, count, edge_pack, 0)
        send_all(b, send_ed, recv_ed, send_sem_ed, recv_sem_ed)
        return carry

    lax.fori_loop(0, stages, stage, 0)

    lane = lax.rem(lax.broadcasted_iota(jnp.int32, (320, PLANE), 1), 2 * HALF)
    real = lane < HALF

    def others(b, ref, send_sem, recv_sem):
        return pltpu.make_async_remote_copy(
            src_ref=ref.at[b, pl.ds(0, count - 1)], dst_ref=ref.at[b, pl.ds(0, count - 1)],
            send_sem=send_sem.at[b], recv_sem=recv_sem.at[b],
            device_id={"tile": below}, device_id_type=pl.DeviceIdType.MESH,
        )

    def finish(b, carry):
        others(b, recv_in, send_sem_in, recv_sem_in).wait_recv()
        others(b, recv_ed, send_sem_ed, recv_sem_ed).wait_recv()

        def lift(s, carry):
            pair = [recv_ed[b, 2 * s + k].astype(jnp.float32) for k in range(2)]
            edge_kx[pl.ds(pl.multiple_of(8 * s, 8), 8), :] = jnp.concatenate(pair, axis=0)
            return carry

        lax.fori_loop(0, count // 2, lift, 0)
        inner = recv_in[b].reshape(count * inner_rows, PLANE)
        edge = edge_kx[...].astype(jnp.bfloat16)
        for h in range(2):
            rows = slice(320 * h, 320 * (h + 1))

            def product(part):
                return jnp.dot(
                    inner_table_ref[part, rows, :], inner, preferred_element_type=jnp.float32
                ) + jnp.dot(edge_table_ref[part, rows, :], edge, preferred_element_type=jnp.float32)

            first = product(0)
            second = product(1)
            ahead = pltpu.roll(second, PLANE - HALF, 1)
            behind = pltpu.roll(second, HALF, 1)
            out = first + jnp.where(real, -ahead, behind)
            at = pl.ds(pl.multiple_of(b * PLANE, PLANE), PLANE)
            out_ref[rows, at] = (out * (1.0 / PLANE)).astype(jnp.bfloat16)
        return carry

    lax.fori_loop(0, stages, finish, 0)

    def sent(b, carry):
        others(b, send_in, send_sem_in, recv_sem_in).wait_send()
        others(b, send_ed, send_sem_ed, recv_sem_ed).wait_send()
        return carry

    lax.fori_loop(0, stages, sent, 0)


def transform_plane(ky_table, inner_table, edge_table, grid, own, up, down):
    stages, count, rows, wide = 5, 32, TILE_ROWS - 4, 2 * LANES
    bf16, f32 = jnp.bfloat16, jnp.float32
    dma = pltpu.SemaphoreType.DMA
    return pl.pallas_call(
        mid_kernel,
        out_shape=jax.ShapeDtypeStruct((PLANE, stages * PLANE), bf16),
        in_specs=[VMEM] * 7,
        out_specs=VMEM,
        scratch_shapes=[
            pltpu.VMEM((stages, count, rows, PLANE), bf16),
            pltpu.VMEM((stages, count, 4, PLANE), bf16),
            pltpu.VMEM((stages, count, rows, PLANE), bf16),
            pltpu.VMEM((stages, count, 4, PLANE), bf16),
            pltpu.VMEM((2, 2, PLANE, wide), bf16),
            pltpu.VMEM((rows, PLANE, wide), bf16),
            pltpu.VMEM((4, PLANE, wide), bf16),
            pltpu.VMEM((4, PLANE, wide), bf16),
            pltpu.VMEM((rows * LANES, LANES), f32),
            pltpu.VMEM((rows * LANES, LANES), f32),
            pltpu.VMEM((4 * count, PLANE), f32),
            dma((2,)), dma((2,)), dma((stages,)), dma((stages,)), dma((stages,)), dma((stages,)),
        ],
        compiler_params=pltpu.CompilerParams(
            vmem_limit_bytes=42 * MB, collective_id=0, has_side_effects=True
        ),
        cost_estimate=pl.CostEstimate(flops=20 * 10**9, bytes_accessed=20 * MB, transcendentals=0),
        name="plane",
    )(ky_table, inner_table, edge_table, grid, own, up, down)


def make_tables():
    idx = np.arange(PLANE)
    phase = (idx[:, None] * idx[None, :] % PLANE).astype(np.float32) * np.float32(2.0 * math.pi / PLANE)
    cos_tab = np.cos(phase).astype(ml_dtypes.bfloat16)
    sin_tab = np.sin(phase).astype(ml_dtypes.bfloat16)
    ky_table = np.concatenate([cos_tab, sin_tab], axis=1)
    ky_table = ky_table.reshape(32, 5, 4, 2 * PLANE).transpose(1, 0, 2, 3).reshape(5, LANES, 2 * PLANE)
    both = np.stack([cos_tab, sin_tab]).reshape(2, PLANE, 32, TILE_ROWS)
    inner_table = both[..., 2:18].reshape(2, PLANE, 512)
    edge_table = np.concatenate([both[..., 0:2], both[..., 18:20]], axis=-1).reshape(2, PLANE, 128)
    return ky_table, inner_table, edge_table


def body(coil_data, frame_of, basis, sample_pos, window_at, live_count):
    devices = 256
    data = coil_data.reshape(devices, 16, 2, LANES)
    coef = basis[frame_of.reshape(-1)].reshape(devices, 1, 2, 10)
    coef = jnp.pad(coef, ((0, 0), (0, 0), (0, 0), (0, LANES - 10)))
    sent = jnp.concatenate([data, coef], axis=1)
    got = lax.all_to_all(sent, ("kz", "tile"), split_axis=0, concat_axis=0, tiled=True)
    data = got[:, :16].reshape(2 * devices, 16, LANES)
    coef = got[:, 16, :, :10].astype(jnp.float32).reshape(-1)
    window = window_at.reshape(2 * devices, 2)
    live = (jnp.arange(2)[None, :] < live_count.reshape(devices, 1)).astype(jnp.float32).reshape(-1)
    pos = sample_pos.reshape(2 * devices, 2, LANES)
    inner, own, up, down = grid_tile(window[:, 0], window[:, 1], live, coef, pos, data)
    ky_table, inner_table, edge_table = [jnp.asarray(t) for t in make_tables()]
    return transform_plane(ky_table, inner_table, edge_table, inner, own, up, down)[None]


def solution(mesh):
    return jax.shard_map(
        body,
        mesh=mesh,
        in_specs=(
            P("kz", "tile", None, None, None, None, None),
            P("kz", "tile", None, None, None),
            P(),
            P("kz", "tile", None, None, None, None, None),
            P("kz", "tile", None, None, None, None),
            P("kz", "tile", None, None),
        ),
        out_specs=P("kz", None, "tile"),
        check_vma=False,
    )
```

```python
import functools
import math

import jax
import jax.numpy as jnp
from jax import lax
from jax.experimental import pallas as pl
from jax.experimental.pallas import tpu as pltpu
from jax.sharding import PartitionSpec as P
import ml_dtypes
import numpy as np

PLANE = 640
WIN_ROWS = 4
WIN_COLS = 32
TILE_ROWS = 20
WIDE = 40
PAD = 680
LANES = 128
HALF = 80
MB = 1024 * 1024


def taper(dist):
    inner = 1.0 - (dist * (1.0 / 1.5)) * (dist * (1.0 / 1.5))
    inner = jnp.maximum(inner, 0.0)
    return inner * inner


def grid_slots(row_ref, col_ref, live_ref, coef_ref, pos_ref, data_ref, acc_ref, batch):
    count = data_ref.shape[0]
    row_cell = lax.broadcasted_iota(jnp.int32, (8, LANES), 0)
    col_cell = lax.broadcasted_iota(jnp.int32, (WIDE, LANES), 0)
    zero = jnp.zeros((LANES - HALF, LANES), jnp.bfloat16)

    def contribution(s):
        col0 = col_ref[s]
        shift = jnp.bitwise_and(col0, 7)
        place = pos_ref[s]
        u = place[0:1, :]
        v = place[1:2, :]
        row_k = taper(row_cell.astype(jnp.float32) - u) * live_ref[s]
        col_k = taper((col_cell - shift).astype(jnp.float32) - v)
        weight = jnp.concatenate([row_k[i : i + 1, :] * col_k for i in range(WIN_ROWS)], axis=0)
        weight = weight.astype(jnp.bfloat16)
        data = data_ref[s].astype(jnp.float32)
        re, im = data[0:8], data[8:16]
        scale = [coef_ref[s * 10 + r] for r in range(10)]
        re = jnp.concatenate([re * c for c in scale], axis=0).astype(jnp.bfloat16)
        im = jnp.concatenate([im * c for c in scale], axis=0).astype(jnp.bfloat16)
        re = jnp.concatenate([re, zero], axis=0)
        im = jnp.concatenate([im, zero], axis=0)
        across = (((1,), (1,)), ((), ()))
        return [
            lax.dot_general(weight, half, across, preferred_element_type=jnp.float32) for half in (re, im)
        ]

    def step(b, carry):
        slots = [b * batch + k for k in range(batch)]
        parts = [contribution(s) for s in slots]
        for s, part in zip(slots, parts):
            row = row_ref[s] + 2
            start = pl.multiple_of(jnp.bitwise_and(col_ref[s], -8), 8)
            for i in range(WIN_ROWS):
                at = (row + i, pl.ds(start, WIDE), slice(None))
                rows = slice(i * WIDE, (i + 1) * WIDE)
                acc_ref[at] += jnp.concatenate([half[rows] for half in part], axis=1)
        return carry

    lax.fori_loop(0, count // batch, step, 0)


def exchange_kernel(data_ref, coef_ref, data_out, coef_out,
                    ready, data_send, data_recv, coef_send, coef_recv, own_sem):
    parts, tiles = lax.axis_size("kz"), lax.axis_size("tile")
    kz, tile = lax.axis_index("kz"), lax.axis_index("tile")
    devices = parts * tiles
    me = kz * tiles + tile
    barrier = pltpu.get_barrier_semaphore()

    def signal(sem, part, spot):
        pl.semaphore_signal(sem, inc=1, device_id=(part, spot), device_id_type=pl.DeviceIdType.MESH)

    def greet_tile(k, carry):
        signal(barrier, kz, lax.rem(tile + k, tiles))
        return carry

    def greet_part(k, carry):
        signal(barrier, lax.rem(kz + k, parts), tile)
        return carry

    def tell_part(k, carry):
        signal(ready, lax.rem(kz + k, parts), tile)
        return carry

    lax.fori_loop(1, tiles, greet_tile, 0)
    lax.fori_loop(1, parts, greet_part, 0)
    pl.semaphore_wait(barrier, tiles + parts - 2)
    lax.fori_loop(1, parts, tell_part, 0)
    pl.semaphore_wait(ready, parts - 1)

    def copies(source, k, target):
        part = lax.rem(kz + k // tiles, parts)
        spot = lax.rem(tile + lax.rem(k, tiles), tiles)
        to = part * tiles + spot
        pairs = ((data_ref, data_out, data_send, data_recv), (coef_ref, coef_out, coef_send, coef_recv))
        return [
            pltpu.make_async_remote_copy(
                src_ref=src.at[source(to)], dst_ref=dst.at[target], send_sem=send, recv_sem=recv,
                device_id=(part, spot), device_id_type=pl.DeviceIdType.MESH,
            )
            for src, dst, send, recv in pairs
        ]

    def send(k, carry):
        for copy in copies(lambda to: to, k, me):
            copy.start()
        return carry

    lax.fori_loop(1, devices, send, 0)
    own = pltpu.make_async_copy(data_ref.at[me], data_out.at[me], own_sem)
    own.start()
    coef_out[me] = coef_ref[me]
    own.wait()
    others = pl.ds(0, devices - 1)
    for copy in copies(lambda to: others, 1, others):
        copy.wait_send()
        copy.wait_recv()


def exchange(data, coef):
    dma = pltpu.SemaphoreType.DMA
    return pl.pallas_call(
        exchange_kernel,
        out_shape=[
            jax.ShapeDtypeStruct(data.shape, data.dtype),
            jax.ShapeDtypeStruct(coef.shape, coef.dtype),
        ],
        in_specs=[ANY, VMEM],
        out_specs=[ANY, VMEM],
        scratch_shapes=[pltpu.SemaphoreType.REGULAR] + [dma] * 5,
        compiler_params=pltpu.CompilerParams(collective_id=1, has_side_effects=True),
        cost_estimate=pl.CostEstimate(flops=0, bytes_accessed=4 * MB, transcendentals=0),
        name="exchange",
    )(data, coef)


def grid_kernel(row_ref, col_ref, live_ref, coef_ref, pos_ref, data_ref,
                inner_ref, own_ref, up_ref, down_ref, acc_ref, *, batch):
    def clear(k, carry):
        acc_ref[k] = jnp.zeros(acc_ref.shape[1:], jnp.float32)
        return carry

    lax.fori_loop(0, acc_ref.shape[0], clear, 0)
    grid_slots(row_ref, col_ref, live_ref, coef_ref, pos_ref, data_ref, acc_ref, batch)

    def row_of(k):
        wrap = acc_ref[k, 0:WIDE, :] + acc_ref[k, PLANE:PAD, :]
        return jnp.concatenate([wrap, acc_ref[k, WIDE:PLANE, :]], axis=0)

    for k in range(2):
        up_ref[k] = row_of(k).astype(jnp.bfloat16)
        down_ref[k] = row_of(TILE_ROWS + 2 + k).astype(jnp.bfloat16)
        own_ref[k] = row_of(2 + k)
        own_ref[2 + k] = row_of(TILE_ROWS + k)

    def emit(k, carry):
        inner_ref[k] = row_of(k + 4).astype(jnp.bfloat16)
        return carry

    lax.fori_loop(0, TILE_ROWS - 4, emit, 0)


SMEM = pl.BlockSpec(memory_space=pltpu.SMEM)
VMEM = pl.BlockSpec(memory_space=pltpu.VMEM)
ANY = pl.BlockSpec(memory_space=pl.ANY)


def grid_tile(rows, cols, live, coef, pos, data, batch=32):
    wide = 2 * LANES
    return pl.pallas_call(
        functools.partial(grid_kernel, batch=batch),
        out_shape=[
            jax.ShapeDtypeStruct((TILE_ROWS - 4, PLANE, wide), jnp.bfloat16),
            jax.ShapeDtypeStruct((4, PLANE, wide), jnp.float32),
            jax.ShapeDtypeStruct((2, PLANE, wide), jnp.bfloat16),
            jax.ShapeDtypeStruct((2, PLANE, wide), jnp.bfloat16),
        ],
        in_specs=[SMEM] * 4 + [VMEM] * 2,
        out_specs=[VMEM] * 4,
        scratch_shapes=[pltpu.VMEM((TILE_ROWS + 4, PAD, wide), jnp.float32)],
        compiler_params=pltpu.CompilerParams(vmem_limit_bytes=40 * MB),
        cost_estimate=pl.CostEstimate(flops=6 * 10**9, bytes_accessed=20 * MB, transcendentals=0),
        name="grid_tile",
    )(rows, cols, live, coef, pos, data)


def interleave(pieces):
    lane = lax.broadcasted_iota(jnp.int32, pieces[0].shape, 1)
    p = [pieces[0]] + [pltpu.roll(pieces[k], (HALF * k) % LANES, 1) for k in range(1, 8)]
    return [
        jnp.where(lane < 80, p[0], p[1]),
        jnp.where(lane < 32, p[1], jnp.where(lane < 112, p[2], p[3])),
        jnp.where(lane < 64, p[3], p[4]),
        jnp.where(lane < 16, p[4], jnp.where(lane < 96, p[5], p[6])),
        jnp.where(lane < 48, p[6], p[7]),
    ]


def mid_kernel(ky_ref, inner_table_ref, edge_table_ref, grid_ref, own_ref, up_ref, down_ref, out_ref,
               send_in, send_ed, recv_in, recv_ed, halo, rot, edge_grid, edge_rot, re_ref, im_ref, edge_kx,
               halo_send, halo_recv, send_sem_in, recv_sem_in, send_sem_ed, recv_sem_ed):
    count = lax.axis_size("tile")
    me = lax.axis_index("tile")
    above = lax.rem(me + count - 1, count)
    below = lax.rem(me + 1, count)
    stages = ky_ref.shape[0]
    inner_rows = TILE_ROWS - 4

    barrier = pltpu.get_barrier_semaphore()

    def greet(k, carry):
        pl.semaphore_signal(
            barrier, inc=1, device_id={"tile": lax.rem(me + k, count)}, device_id_type=pl.DeviceIdType.MESH
        )
        return carry

    lax.fori_loop(1, count, greet, 0)
    pl.semaphore_wait(barrier, count - 1)

    def halo_copy(source, way, peer):
        return pltpu.make_async_remote_copy(
            src_ref=source, dst_ref=halo.at[way], send_sem=halo_send.at[way], recv_sem=halo_recv.at[way],
            device_id={"tile": peer}, device_id_type=pl.DeviceIdType.MESH,
        )

    to_below = halo_copy(down_ref, 0, below)
    to_above = halo_copy(up_ref, 1, above)
    to_below.start()
    to_above.start()

    def turned(plane):
        return jnp.concatenate([-plane[:, LANES:], plane[:, :LANES]], axis=1)

    def turn(k, carry):
        rot[k] = turned(grid_ref[k])
        return carry

    lax.fori_loop(0, inner_rows, turn, 0)

    def rows_of(b, k, plane_ref, turned_ref):
        out = jnp.dot(ky_ref[b, :, :PLANE], plane_ref[k], preferred_element_type=jnp.float32)
        out += jnp.dot(ky_ref[b, :, PLANE:], turned_ref[k], preferred_element_type=jnp.float32)
        at = pl.ds(pl.multiple_of(k * LANES, LANES), LANES)
        re_ref[at, :] = out[:, :LANES]
        im_ref[at, :] = out[:, LANES:]

    def pieces_of(start, size):
        pieces = []
        for j in range(4):
            at = pl.ds(start + j, size, stride=LANES)
            pieces += [re_ref[at, :], im_ref[at, :]]
        return jnp.concatenate(interleave(pieces), axis=1)

    def send_all(b, send, recv, send_sem, recv_sem):
        recv[b, me] = send[b, me]

        def to_peer(k, carry):
            peer = lax.rem(me + k, count)
            pltpu.make_async_remote_copy(
                src_ref=send.at[b, peer], dst_ref=recv.at[b, me],
                send_sem=send_sem.at[b], recv_sem=recv_sem.at[b],
                device_id={"tile": peer}, device_id_type=pl.DeviceIdType.MESH,
            ).start()
            return carry

        lax.fori_loop(1, count, to_peer, 0)

    def stage(b, carry):
        def inner_row(k, carry):
            rows_of(b, k, grid_ref, rot)
            return carry

        lax.fori_loop(0, inner_rows, inner_row, 0)

        def inner_pack(d, carry):
            halves = [pieces_of(g * 8 * LANES + d * 4, 8) for g in range(2)]
            send_in[b, d] = jnp.concatenate(halves, axis=0).astype(jnp.bfloat16)
            return carry

        lax.fori_loop(0, count, inner_pack, 0)
        send_all(b, send_in, recv_in, send_sem_in, recv_sem_in)

        @pl.when(b == 0)
        def _():
            to_below.wait()
            to_above.wait()
            for k in range(2):
                edge_grid[k] = (own_ref[k] + halo[0, k].astype(jnp.float32)).astype(jnp.bfloat16)
                edge_grid[2 + k] = (own_ref[2 + k] + halo[1, k].astype(jnp.float32)).astype(jnp.bfloat16)
            for k in range(4):
                edge_rot[k] = turned(edge_grid[k])

        def edge_row(k, carry):
            rows_of(b, k, edge_grid, edge_rot)
            return carry

        lax.fori_loop(0, 4, edge_row, 0)

        def edge_pack(d, carry):
            send_ed[b, d] = pieces_of(d * 4, 4).astype(jnp.bfloat16)
            return carry

        lax.fori_loop(0, count, edge_pack, 0)
        send_all(b, send_ed, recv_ed, send_sem_ed, recv_sem_ed)
        return carry

    lax.fori_loop(0, stages, stage, 0)

    lane = lax.rem(lax.broadcasted_iota(jnp.int32, (320, PLANE), 1), 2 * HALF)
    real = lane < HALF

    def others(b, ref, send_sem, recv_sem):
        return pltpu.make_async_remote_copy(
            src_ref=ref.at[b, pl.ds(0, count - 1)], dst_ref=ref.at[b, pl.ds(0, count - 1)],
            send_sem=send_sem.at[b], recv_sem=recv_sem.at[b],
            device_id={"tile": below}, device_id_type=pl.DeviceIdType.MESH,
        )

    def finish(b, carry):
        others(b, recv_in, send_sem_in, recv_sem_in).wait_recv()
        others(b, recv_ed, send_sem_ed, recv_sem_ed).wait_recv()

        def lift(s, carry):
            pair = [recv_ed[b, 2 * s + k].astype(jnp.float32) for k in range(2)]
            edge_kx[pl.ds(pl.multiple_of(8 * s, 8), 8), :] = jnp.concatenate(pair, axis=0)
            return carry

        lax.fori_loop(0, count // 2, lift, 0)
        inner = recv_in[b].reshape(count * inner_rows, PLANE)
        edge = edge_kx[...].astype(jnp.bfloat16)
        for h in range(2):
            rows = slice(320 * h, 320 * (h + 1))

            def product(part):
                return jnp.dot(
                    inner_table_ref[part, rows, :], inner, preferred_element_type=jnp.float32
                ) + jnp.dot(edge_table_ref[part, rows, :], edge, preferred_element_type=jnp.float32)

            first = product(0)
            second = product(1)
            ahead = pltpu.roll(second, PLANE - HALF, 1)
            behind = pltpu.roll(second, HALF, 1)
            out = first + jnp.where(real, -ahead, behind)
            at = pl.ds(pl.multiple_of(b * PLANE, PLANE), PLANE)
            out_ref[rows, at] = (out * (1.0 / PLANE)).astype(jnp.bfloat16)
        return carry

    lax.fori_loop(0, stages, finish, 0)

    def sent(b, carry):
        others(b, send_in, send_sem_in, recv_sem_in).wait_send()
        others(b, send_ed, send_sem_ed, recv_sem_ed).wait_send()
        return carry

    lax.fori_loop(0, stages, sent, 0)


def transform_plane(ky_table, inner_table, edge_table, grid, own, up, down):
    stages, count, rows, wide = 5, 32, TILE_ROWS - 4, 2 * LANES
    bf16, f32 = jnp.bfloat16, jnp.float32
    dma = pltpu.SemaphoreType.DMA
    return pl.pallas_call(
        mid_kernel,
        out_shape=jax.ShapeDtypeStruct((PLANE, stages * PLANE), bf16),
        in_specs=[VMEM] * 7,
        out_specs=VMEM,
        scratch_shapes=[
            pltpu.VMEM((stages, count, rows, PLANE), bf16),
            pltpu.VMEM((stages, count, 4, PLANE), bf16),
            pltpu.VMEM((stages, count, rows, PLANE), bf16),
            pltpu.VMEM((stages, count, 4, PLANE), bf16),
            pltpu.VMEM((2, 2, PLANE, wide), bf16),
            pltpu.VMEM((rows, PLANE, wide), bf16),
            pltpu.VMEM((4, PLANE, wide), bf16),
            pltpu.VMEM((4, PLANE, wide), bf16),
            pltpu.VMEM((rows * LANES, LANES), f32),
            pltpu.VMEM((rows * LANES, LANES), f32),
            pltpu.VMEM((4 * count, PLANE), f32),
            dma((2,)), dma((2,)), dma((stages,)), dma((stages,)), dma((stages,)), dma((stages,)),
        ],
        compiler_params=pltpu.CompilerParams(
            vmem_limit_bytes=36 * MB, collective_id=0, has_side_effects=True
        ),
        cost_estimate=pl.CostEstimate(flops=20 * 10**9, bytes_accessed=20 * MB, transcendentals=0),
        name="plane",
    )(ky_table, inner_table, edge_table, grid, own, up, down)


def make_tables():
    idx = np.arange(PLANE)
    phase = (idx[:, None] * idx[None, :] % PLANE).astype(np.float32) * np.float32(2.0 * math.pi / PLANE)
    cos_tab = np.cos(phase).astype(ml_dtypes.bfloat16)
    sin_tab = np.sin(phase).astype(ml_dtypes.bfloat16)
    ky_table = np.concatenate([cos_tab, sin_tab], axis=1)
    ky_table = ky_table.reshape(32, 5, 4, 2 * PLANE).transpose(1, 0, 2, 3).reshape(5, LANES, 2 * PLANE)
    both = np.stack([cos_tab, sin_tab]).reshape(2, PLANE, 32, TILE_ROWS)
    inner_table = both[..., 2:18].reshape(2, PLANE, 512)
    edge_table = np.concatenate([both[..., 0:2], both[..., 18:20]], axis=-1).reshape(2, PLANE, 128)
    return ky_table, inner_table, edge_table


def body(coil_data, frame_of, basis, sample_pos, window_at, live_count):
    devices = 256
    coef = basis[frame_of.reshape(-1)].astype(jnp.float32).reshape(devices, 1, 20)
    coef = jnp.pad(coef, ((0, 0), (0, 0), (0, LANES - 20)))
    data, coef = exchange(coil_data.reshape(devices, 32, LANES), coef)
    data = data.reshape(2 * devices, 16, LANES)
    coef = coef[:, 0, :20].reshape(-1)
    window = window_at.reshape(2 * devices, 2)
    live = (jnp.arange(2)[None, :] < live_count.reshape(devices, 1)).astype(jnp.float32).reshape(-1)
    pos = sample_pos.reshape(2 * devices, 2, LANES)
    inner, own, up, down = grid_tile(window[:, 0], window[:, 1], live, coef, pos, data)
    ky_table, inner_table, edge_table = [jnp.asarray(t) for t in make_tables()]
    return transform_plane(ky_table, inner_table, edge_table, inner, own, up, down)[None]


def solution(mesh):
    return jax.shard_map(
        body,
        mesh=mesh,
        in_specs=(
            P("kz", "tile", None, None, None, None, None),
            P("kz", "tile", None, None, None),
            P(),
            P("kz", "tile", None, None, None, None, None),
            P("kz", "tile", None, None, None, None),
            P("kz", "tile", None, None),
        ),
        out_specs=P("kz", None, "tile"),
        check_vma=False,
    )
```

```python
import functools
import math

import jax
import jax.numpy as jnp
from jax import lax
from jax.experimental import pallas as pl
from jax.experimental.pallas import tpu as pltpu
from jax.sharding import PartitionSpec as P
import ml_dtypes
import numpy as np

PLANE = 640
WIN_ROWS = 4
WIN_COLS = 32
TILE_ROWS = 20
PAD = PLANE + WIN_COLS
LANES = 128
HALF = 80
RANK = 10
MB = 1024 * 1024


def taper(dist):
    inner = 1.0 - (dist * (1.0 / 1.5)) * (dist * (1.0 / 1.5))
    inner = jnp.maximum(inner, 0.0)
    return inner * inner


SMEM = pl.BlockSpec(memory_space=pltpu.SMEM)
VMEM = pl.BlockSpec(memory_space=pltpu.VMEM)
HBM = pl.BlockSpec(memory_space=pltpu.HBM)


def exchange_kernel(frame_ref, basis_ref, data_ref, data_out, coef_out,
                    coef_ref, ready, data_send, data_recv, coef_send, coef_recv, own_sem):
    parts, tiles = lax.axis_size("kz"), lax.axis_size("tile")
    kz, tile = lax.axis_index("kz"), lax.axis_index("tile")
    devices = parts * tiles
    me = kz * tiles + tile
    barrier = pltpu.get_barrier_semaphore()

    def signal(sem, part, spot):
        pl.semaphore_signal(sem, inc=1, device_id=(part, spot), device_id_type=pl.DeviceIdType.MESH)

    def greet_tile(k, carry):
        signal(barrier, kz, lax.rem(tile + k, tiles))
        return carry

    def greet_part(k, carry):
        signal(barrier, lax.rem(kz + k, parts), tile)
        return carry

    def tell_part(k, carry):
        signal(ready, lax.rem(kz + k, parts), tile)
        return carry

    lax.fori_loop(1, tiles, greet_tile, 0)
    lax.fori_loop(1, parts, greet_part, 0)
    pl.semaphore_wait(barrier, tiles + parts - 2)
    lax.fori_loop(1, parts, tell_part, 0)
    pl.semaphore_wait(ready, parts - 1)

    def copies(pair, source, k, target):
        part = lax.rem(kz + k // tiles, parts)
        spot = lax.rem(tile + lax.rem(k, tiles), tiles)
        src, dst, send, recv = pair
        return pltpu.make_async_remote_copy(
            src_ref=src.at[source(part * tiles + spot)], dst_ref=dst.at[target], send_sem=send, recv_sem=recv,
            device_id=(part, spot), device_id_type=pl.DeviceIdType.MESH,
        )

    def send_all(pair):
        def send(k, carry):
            copies(pair, lambda to: to, k, me).start()
            return carry

        lax.fori_loop(1, devices, send, 0)

    data = (data_ref, data_out, data_send, data_recv)
    coef = (coef_ref, coef_out, coef_send, coef_recv)
    send_all(data)
    lane = lax.broadcasted_iota(jnp.int32, (1, 2 * RANK), 1)

    def look_up(p, carry):
        first, second = [basis_ref[pl.ds(frame_ref[p // tiles, s, lax.rem(p, tiles)], 1), :] for s in range(2)]
        coef_ref[p] = jnp.where(lane < RANK, first, second)
        return carry

    lax.fori_loop(0, devices, look_up, 0, unroll=8)
    send_all(coef)
    own = pltpu.make_async_copy(data_ref.at[me], data_out.at[me], own_sem)
    own.start()
    coef_out[me] = coef_ref[me]
    own.wait()
    others = pl.ds(0, devices - 1)
    for pair in (data, coef):
        every = copies(pair, lambda to: others, 1, others)
        every.wait_send()
        every.wait_recv()


def exchange(frames, table, data):
    dma = pltpu.SemaphoreType.DMA
    devices = data.shape[0]
    return pl.pallas_call(
        exchange_kernel,
        out_shape=[
            jax.ShapeDtypeStruct(data.shape, data.dtype),
            jax.ShapeDtypeStruct((devices, 1, 2 * RANK), jnp.float32),
        ],
        in_specs=[SMEM, VMEM, HBM],
        out_specs=[VMEM, VMEM],
        scratch_shapes=[pltpu.VMEM((devices, 1, 2 * RANK), jnp.float32), pltpu.SemaphoreType.REGULAR] + [dma] * 5,
        compiler_params=pltpu.CompilerParams(collective_id=1, has_side_effects=True, vmem_limit_bytes=8 * MB),
        cost_estimate=pl.CostEstimate(flops=0, bytes_accessed=4 * MB, transcendentals=0),
        name="exchange",
    )(frames, table, data)


def grid_slots(window_ref, live_ref, coef_ref, pos_ref, data_ref, acc_ref):
    parts, slots, _, tiles = window_ref.shape
    row_cell = lax.broadcasted_iota(jnp.int32, (8, LANES), 0).astype(jnp.float32)
    col_cell = lax.broadcasted_iota(jnp.int32, (WIN_COLS, LANES), 0).astype(jnp.float32)
    zero = jnp.zeros((LANES - HALF, LANES), jnp.bfloat16)

    def contribution(a, t, s):
        pair = a * tiles + t
        place = pos_ref[pair * slots + s]
        living = (s < live_ref[a, t]).astype(jnp.float32)
        row_k = taper(row_cell - place[0:1, :]) * living
        col_k = taper(col_cell - place[1:2, :])
        weight = jnp.concatenate([row_k[i : i + 1, :] * col_k for i in range(WIN_ROWS)], axis=0)
        weight = weight.astype(jnp.bfloat16)
        data = data_ref[pair, 16 * s : 16 * (s + 1)].astype(jnp.float32)
        scale = [coef_ref[pair, 0, s * 10 + r] for r in range(10)]
        across = (((1,), (1,)), ((), ()))
        halves = []
        for half in (data[0:8], data[8:16]):
            values = jnp.concatenate([half * c for c in scale], axis=0).astype(jnp.bfloat16)
            values = jnp.concatenate([values, zero], axis=0)
            halves.append(lax.dot_general(weight, values, across, preferred_element_type=jnp.float32))
        return halves

    def step(a, carry):
        slot_ids = [(t, s) for t in range(tiles) for s in range(slots)]
        sums = [contribution(a, t, s) for t, s in slot_ids]
        for (t, s), halves in zip(slot_ids, sums):
            row = window_ref[a, s, 0, t] + 2
            col = window_ref[a, s, 1, t]
            for i in range(WIN_ROWS):
                for h, half in enumerate(halves):
                    at = (h, row + i, pl.ds(col, WIN_COLS), slice(None))
                    acc_ref[at] += half[i * WIN_COLS : (i + 1) * WIN_COLS]
        return carry

    lax.fori_loop(0, parts, step, 0)


def grid_kernel(window_ref, live_ref, coef_ref, pos_ref, data_ref,
                inner_ref, own_ref, up_ref, down_ref, acc_ref):
    def clear(k, carry):
        for h in range(2):
            acc_ref[h, k] = jnp.zeros(acc_ref.shape[2:], jnp.float32)
        return carry

    lax.fori_loop(0, acc_ref.shape[1], clear, 0)
    grid_slots(window_ref, live_ref, coef_ref, pos_ref, data_ref, acc_ref)

    def put(out_ref, k, row):
        for h in range(2):
            lanes = slice(h * LANES, (h + 1) * LANES)
            wrap = acc_ref[h, row, 0:WIN_COLS, :] + acc_ref[h, row, PLANE:PAD, :]
            out_ref[k, 0:WIN_COLS, lanes] = wrap.astype(out_ref.dtype)
            out_ref[k, WIN_COLS:PLANE, lanes] = acc_ref[h, row, WIN_COLS:PLANE, :].astype(out_ref.dtype)

    for k in range(2):
        put(up_ref, k, k)
        put(down_ref, k, TILE_ROWS + 2 + k)
        put(own_ref, k, 2 + k)
        put(own_ref, 2 + k, TILE_ROWS + k)

    def emit(k, carry):
        put(inner_ref, k, k + 4)
        return carry

    lax.fori_loop(0, TILE_ROWS - 4, emit, 0)


def grid_tile(window, live, coef, pos, data):
    wide = 2 * LANES
    return pl.pallas_call(
        grid_kernel,
        out_shape=[
            jax.ShapeDtypeStruct((TILE_ROWS - 4, PLANE, wide), jnp.bfloat16),
            jax.ShapeDtypeStruct((4, PLANE, wide), jnp.float32),
            jax.ShapeDtypeStruct((2, PLANE, wide), jnp.bfloat16),
            jax.ShapeDtypeStruct((2, PLANE, wide), jnp.bfloat16),
        ],
        in_specs=[SMEM] * 3 + [VMEM] * 2,
        out_specs=[VMEM] * 4,
        scratch_shapes=[pltpu.VMEM((2, TILE_ROWS + 4, PAD, LANES), jnp.float32)],
        compiler_params=pltpu.CompilerParams(vmem_limit_bytes=40 * MB),
        cost_estimate=pl.CostEstimate(flops=6 * 10**9, bytes_accessed=20 * MB, transcendentals=0),
        name="grid_tile",
    )(window, live, coef, pos, data)


def interleave(pieces):
    lane = lax.broadcasted_iota(jnp.int32, pieces[0].shape, 1)
    p = [pieces[0]] + [pltpu.roll(pieces[k], (HALF * k) % LANES, 1) for k in range(1, 8)]
    return [
        jnp.where(lane < 80, p[0], p[1]),
        jnp.where(lane < 32, p[1], jnp.where(lane < 112, p[2], p[3])),
        jnp.where(lane < 64, p[3], p[4]),
        jnp.where(lane < 16, p[4], jnp.where(lane < 96, p[5], p[6])),
        jnp.where(lane < 48, p[6], p[7]),
    ]


def mid_kernel(ky_ref, inner_table_ref, edge_table_ref, grid_ref, own_ref, up_ref, down_ref, out_ref,
               send_in, send_ed, recv_in, recv_ed, halo, rot, edge_grid, edge_rot, re_ref, im_ref, edge_kx,
               halo_send, halo_recv, send_sem_in, recv_sem_in, send_sem_ed, recv_sem_ed):
    count = lax.axis_size("tile")
    me = lax.axis_index("tile")
    above = lax.rem(me + count - 1, count)
    below = lax.rem(me + 1, count)
    stages = ky_ref.shape[0]
    inner_rows = TILE_ROWS - 4

    barrier = pltpu.get_barrier_semaphore()

    def greet(k, carry):
        pl.semaphore_signal(
            barrier, inc=1, device_id={"tile": lax.rem(me + k, count)}, device_id_type=pl.DeviceIdType.MESH
        )
        return carry

    lax.fori_loop(1, count, greet, 0)
    pl.semaphore_wait(barrier, count - 1)

    def halo_copy(source, way, peer):
        return pltpu.make_async_remote_copy(
            src_ref=source, dst_ref=halo.at[way], send_sem=halo_send.at[way], recv_sem=halo_recv.at[way],
            device_id={"tile": peer}, device_id_type=pl.DeviceIdType.MESH,
        )

    to_below = halo_copy(down_ref, 0, below)
    to_above = halo_copy(up_ref, 1, above)
    to_below.start()
    to_above.start()

    def turned(plane):
        return jnp.concatenate([-plane[:, LANES:], plane[:, :LANES]], axis=1)

    def turn(k, carry):
        rot[k] = turned(grid_ref[k])
        return carry

    lax.fori_loop(0, inner_rows, turn, 0)

    def rows_of(b, k, plane_ref, turned_ref):
        out = jnp.dot(ky_ref[b, :, :PLANE], plane_ref[k], preferred_element_type=jnp.float32)
        out += jnp.dot(ky_ref[b, :, PLANE:], turned_ref[k], preferred_element_type=jnp.float32)
        at = pl.ds(pl.multiple_of(k * LANES, LANES), LANES)
        re_ref[at, :] = out[:, :LANES]
        im_ref[at, :] = out[:, LANES:]

    def pieces_of(start, size):
        pieces = []
        for j in range(4):
            at = pl.ds(start + j, size, stride=LANES)
            pieces += [re_ref[at, :], im_ref[at, :]]
        return jnp.concatenate(interleave(pieces), axis=1)

    def send_all(b, send, recv, send_sem, recv_sem):
        recv[b, me] = send[b, me]

        def to_peer(k, carry):
            peer = lax.rem(me + k, count)
            pltpu.make_async_remote_copy(
                src_ref=send.at[b, peer], dst_ref=recv.at[b, me],
                send_sem=send_sem.at[b], recv_sem=recv_sem.at[b],
                device_id={"tile": peer}, device_id_type=pl.DeviceIdType.MESH,
            ).start()
            return carry

        lax.fori_loop(1, count, to_peer, 0)

    def stage(b, carry):
        def inner_row(k, carry):
            rows_of(b, k, grid_ref, rot)
            return carry

        lax.fori_loop(0, inner_rows, inner_row, 0, unroll=4)

        def inner_pack(d, carry):
            halves = [pieces_of(g * 8 * LANES + d * 4, 8) for g in range(2)]
            send_in[b, d] = jnp.concatenate(halves, axis=0).astype(jnp.bfloat16)
            return carry

        lax.fori_loop(0, count, inner_pack, 0, unroll=4)
        send_all(b, send_in, recv_in, send_sem_in, recv_sem_in)

        @pl.when(b == 0)
        def _():
            to_below.wait()
            to_above.wait()
            for k in range(2):
                edge_grid[k] = (own_ref[k] + halo[0, k].astype(jnp.float32)).astype(jnp.bfloat16)
                edge_grid[2 + k] = (own_ref[2 + k] + halo[1, k].astype(jnp.float32)).astype(jnp.bfloat16)
            for k in range(4):
                edge_rot[k] = turned(edge_grid[k])

        def edge_row(k, carry):
            rows_of(b, k, edge_grid, edge_rot)
            return carry

        lax.fori_loop(0, 4, edge_row, 0, unroll=4)

        def edge_pack(d, carry):
            send_ed[b, d] = pieces_of(d * 4, 4).astype(jnp.bfloat16)
            return carry

        lax.fori_loop(0, count, edge_pack, 0, unroll=4)
        send_all(b, send_ed, recv_ed, send_sem_ed, recv_sem_ed)
        return carry

    lax.fori_loop(0, stages, stage, 0)

    lane = lax.rem(lax.broadcasted_iota(jnp.int32, (320, PLANE), 1), 2 * HALF)
    real = lane < HALF

    def others(b, ref, send_sem, recv_sem):
        return pltpu.make_async_remote_copy(
            src_ref=ref.at[b, pl.ds(0, count - 1)], dst_ref=ref.at[b, pl.ds(0, count - 1)],
            send_sem=send_sem.at[b], recv_sem=recv_sem.at[b],
            device_id={"tile": below}, device_id_type=pl.DeviceIdType.MESH,
        )

    def finish(b, carry):
        others(b, recv_in, send_sem_in, recv_sem_in).wait_recv()
        others(b, recv_ed, send_sem_ed, recv_sem_ed).wait_recv()

        def lift(s, carry):
            pair = [recv_ed[b, 2 * s + k].astype(jnp.float32) for k in range(2)]
            edge_kx[pl.ds(pl.multiple_of(8 * s, 8), 8), :] = jnp.concatenate(pair, axis=0)
            return carry

        lax.fori_loop(0, count // 2, lift, 0)
        inner = recv_in[b].reshape(count * inner_rows, PLANE)
        edge = edge_kx[...].astype(jnp.bfloat16)
        for h in range(2):
            rows = slice(320 * h, 320 * (h + 1))

            def product(part):
                return jnp.dot(
                    inner_table_ref[part, rows, :], inner, preferred_element_type=jnp.float32
                ) + jnp.dot(edge_table_ref[part, rows, :], edge, preferred_element_type=jnp.float32)

            first = product(0)
            second = product(1)
            ahead = pltpu.roll(second, PLANE - HALF, 1)
            behind = pltpu.roll(second, HALF, 1)
            out = first + jnp.where(real, -ahead, behind)
            at = pl.ds(pl.multiple_of(b * PLANE, PLANE), PLANE)
            out_ref[rows, at] = (out * (1.0 / PLANE)).astype(jnp.bfloat16)
        return carry

    lax.fori_loop(0, stages, finish, 0)

    def sent(b, carry):
        others(b, send_in, send_sem_in, recv_sem_in).wait_send()
        others(b, send_ed, send_sem_ed, recv_sem_ed).wait_send()
        return carry

    lax.fori_loop(0, stages, sent, 0)


def transform_plane(ky_table, inner_table, edge_table, grid, own, up, down):
    stages, count, rows, wide = 5, 32, TILE_ROWS - 4, 2 * LANES
    bf16, f32 = jnp.bfloat16, jnp.float32
    dma = pltpu.SemaphoreType.DMA
    return pl.pallas_call(
        mid_kernel,
        out_shape=jax.ShapeDtypeStruct((PLANE, stages * PLANE), bf16),
        in_specs=[VMEM] * 7,
        out_specs=VMEM,
        scratch_shapes=[
            pltpu.VMEM((stages, count, rows, PLANE), bf16),
            pltpu.VMEM((stages, count, 4, PLANE), bf16),
            pltpu.VMEM((stages, count, rows, PLANE), bf16),
            pltpu.VMEM((stages, count, 4, PLANE), bf16),
            pltpu.VMEM((2, 2, PLANE, wide), bf16),
            pltpu.VMEM((rows, PLANE, wide), bf16),
            pltpu.VMEM((4, PLANE, wide), bf16),
            pltpu.VMEM((4, PLANE, wide), bf16),
            pltpu.VMEM((rows * LANES, LANES), f32),
            pltpu.VMEM((rows * LANES, LANES), f32),
            pltpu.VMEM((4 * count, PLANE), f32),
            dma((2,)), dma((2,)), dma((stages,)), dma((stages,)), dma((stages,)), dma((stages,)),
        ],
        compiler_params=pltpu.CompilerParams(
            vmem_limit_bytes=36 * MB, collective_id=0, has_side_effects=True
        ),
        cost_estimate=pl.CostEstimate(flops=20 * 10**9, bytes_accessed=20 * MB, transcendentals=0),
        name="plane",
    )(ky_table, inner_table, edge_table, grid, own, up, down)


def make_tables():
    idx = np.arange(PLANE)
    phase = (idx[:, None] * idx[None, :] % PLANE).astype(np.float32) * np.float32(2.0 * math.pi / PLANE)
    cos_tab = np.cos(phase).astype(ml_dtypes.bfloat16)
    sin_tab = np.sin(phase).astype(ml_dtypes.bfloat16)
    ky_table = np.concatenate([cos_tab, sin_tab], axis=1)
    ky_table = ky_table.reshape(32, 5, 4, 2 * PLANE).transpose(1, 0, 2, 3).reshape(5, LANES, 2 * PLANE)
    both = np.stack([cos_tab, sin_tab]).reshape(2, PLANE, 32, TILE_ROWS)
    inner_table = both[..., 2:18].reshape(2, PLANE, 512)
    edge_table = np.concatenate([both[..., 0:2], both[..., 18:20]], axis=-1).reshape(2, PLANE, 128)
    return ky_table, inner_table, edge_table


def body(coil_data, frame_of, basis, sample_pos, window_at, live_count):
    parts, tiles, slots, pair, samples = coil_data.shape[2:]
    devices = parts * tiles
    frames = frame_of[0, 0].transpose(0, 2, 1)
    table = jnp.concatenate([basis, basis], axis=1).astype(jnp.float32)
    data, coef = exchange(frames, table, coil_data.reshape(devices, slots * pair, samples))
    window = window_at[0, 0].transpose(0, 2, 3, 1)
    pos = sample_pos.reshape(devices * slots, 2, samples)
    inner, own, up, down = grid_tile(window, live_count[0, 0], coef, pos, data)
    ky_table, inner_table, edge_table = [jnp.asarray(t) for t in make_tables()]
    return transform_plane(ky_table, inner_table, edge_table, inner, own, up, down)[None]


def solution(mesh):
    return jax.shard_map(
        body,
        mesh=mesh,
        in_specs=(
            P("kz", "tile", None, None, None, None, None),
            P("kz", "tile", None, None, None),
            P(),
            P("kz", "tile", None, None, None, None, None),
            P("kz", "tile", None, None, None, None),
            P("kz", "tile", None, None),
        ),
        out_specs=P("kz", None, "tile"),
        check_vma=False,
    )
```

```python
import functools
import math

import jax
import jax.numpy as jnp
from jax import lax
from jax.experimental import pallas as pl
from jax.experimental.pallas import tpu as pltpu
from jax.sharding import PartitionSpec as P
import ml_dtypes
import numpy as np

PLANE = 640
WIN_ROWS = 4
WIN_COLS = 32
TILE_ROWS = 20
PAD = PLANE + WIN_COLS
LANES = 128
HALF = 80
QUARTER = PLANE // 4
RANK = 10
MB = 1024 * 1024


def taper(dist):
    inner = 1.0 - (dist * (1.0 / 1.5)) * (dist * (1.0 / 1.5))
    inner = jnp.maximum(inner, 0.0)
    return inner * inner


SMEM = pl.BlockSpec(memory_space=pltpu.SMEM)
VMEM = pl.BlockSpec(memory_space=pltpu.VMEM)
HBM = pl.BlockSpec(memory_space=pltpu.HBM)


def exchange_kernel(frame_ref, basis_ref, data_ref, data_out, coef_out,
                    coef_ref, ready, data_send, data_recv, coef_send, coef_recv, own_sem):
    parts, tiles = lax.axis_size("kz"), lax.axis_size("tile")
    kz, tile = lax.axis_index("kz"), lax.axis_index("tile")
    devices = parts * tiles
    me = kz * tiles + tile
    barrier = pltpu.get_barrier_semaphore()

    def signal(sem, part, spot):
        pl.semaphore_signal(sem, inc=1, device_id=(part, spot), device_id_type=pl.DeviceIdType.MESH)

    def greet_tile(k, carry):
        signal(barrier, kz, lax.rem(tile + k, tiles))
        return carry

    def greet_part(k, carry):
        signal(barrier, lax.rem(kz + k, parts), tile)
        return carry

    def tell_part(k, carry):
        signal(ready, lax.rem(kz + k, parts), tile)
        return carry

    lax.fori_loop(1, tiles, greet_tile, 0)
    lax.fori_loop(1, parts, greet_part, 0)
    pl.semaphore_wait(barrier, tiles + parts - 2)
    lax.fori_loop(1, parts, tell_part, 0)
    pl.semaphore_wait(ready, parts - 1)

    def copies(pair, source, k, target):
        part = lax.rem(kz + k // tiles, parts)
        spot = lax.rem(tile + lax.rem(k, tiles), tiles)
        src, dst, send, recv = pair
        return pltpu.make_async_remote_copy(
            src_ref=src.at[source(part * tiles + spot)], dst_ref=dst.at[target], send_sem=send, recv_sem=recv,
            device_id=(part, spot), device_id_type=pl.DeviceIdType.MESH,
        )

    def send_all(pair):
        def send(k, carry):
            copies(pair, lambda to: to, k, me).start()
            return carry

        lax.fori_loop(1, devices, send, 0)

    data = (data_ref, data_out, data_send, data_recv)
    coef = (coef_ref, coef_out, coef_send, coef_recv)
    send_all(data)
    lane = lax.broadcasted_iota(jnp.int32, (1, 2 * RANK), 1)

    def look_up(p, carry):
        first, second = [basis_ref[pl.ds(frame_ref[p // tiles, s, lax.rem(p, tiles)], 1), :] for s in range(2)]
        coef_ref[p] = jnp.where(lane < RANK, first, second)
        return carry

    lax.fori_loop(0, devices, look_up, 0, unroll=8)
    send_all(coef)
    own = pltpu.make_async_copy(data_ref.at[me], data_out.at[me], own_sem)
    own.start()
    coef_out[me] = coef_ref[me]
    own.wait()
    others = pl.ds(0, devices - 1)
    for pair in (data, coef):
        every = copies(pair, lambda to: others, 1, others)
        every.wait_send()
        every.wait_recv()


def exchange(frames, table, data):
    dma = pltpu.SemaphoreType.DMA
    devices = data.shape[0]
    return pl.pallas_call(
        exchange_kernel,
        out_shape=[
            jax.ShapeDtypeStruct(data.shape, data.dtype),
            jax.ShapeDtypeStruct((devices, 1, 2 * RANK), jnp.float32),
        ],
        in_specs=[SMEM, VMEM, HBM],
        out_specs=[VMEM, VMEM],
        scratch_shapes=[pltpu.VMEM((devices, 1, 2 * RANK), jnp.float32), pltpu.SemaphoreType.REGULAR] + [dma] * 5,
        compiler_params=pltpu.CompilerParams(collective_id=1, has_side_effects=True, vmem_limit_bytes=8 * MB),
        cost_estimate=pl.CostEstimate(flops=0, bytes_accessed=4 * MB, transcendentals=0),
        name="exchange",
    )(frames, table, data)


def grid_slots(window_ref, live_ref, coef_ref, pos_ref, data_ref, acc_ref):
    parts, slots, _, tiles = window_ref.shape
    row_cell = lax.broadcasted_iota(jnp.int32, (8, LANES), 0).astype(jnp.float32)
    col_cell = lax.broadcasted_iota(jnp.int32, (WIN_COLS, LANES), 0).astype(jnp.float32)
    zero = jnp.zeros((LANES - HALF, LANES), jnp.bfloat16)

    def contribution(a, t, s):
        pair = a * tiles + t
        place = pos_ref[pair * slots + s]
        living = (s < live_ref[a, t]).astype(jnp.float32)
        row_k = taper(row_cell - place[0:1, :]) * living
        col_k = taper(col_cell - place[1:2, :])
        weight = jnp.concatenate([row_k[i : i + 1, :] * col_k for i in range(WIN_ROWS)], axis=0)
        weight = weight.astype(jnp.bfloat16)
        data = data_ref[pair, 16 * s : 16 * (s + 1)].astype(jnp.float32)
        scale = [coef_ref[pair, 0, s * 10 + r] for r in range(10)]
        across = (((1,), (1,)), ((), ()))
        halves = []
        for half in (data[0:8], data[8:16]):
            values = jnp.concatenate([half * c for c in scale], axis=0).astype(jnp.bfloat16)
            values = jnp.concatenate([values, zero], axis=0)
            halves.append(lax.dot_general(weight, values, across, preferred_element_type=jnp.float32))
        return halves

    def step(a, carry):
        slot_ids = [(t, s) for t in range(tiles) for s in range(slots)]
        sums = [contribution(a, t, s) for t, s in slot_ids]
        for (t, s), halves in zip(slot_ids, sums):
            row = window_ref[a, s, 0, t] + 2
            col = window_ref[a, s, 1, t]
            for i in range(WIN_ROWS):
                for h, half in enumerate(halves):
                    at = (h, row + i, pl.ds(col, WIN_COLS), slice(None))
                    acc_ref[at] += half[i * WIN_COLS : (i + 1) * WIN_COLS]
        return carry

    lax.fori_loop(0, parts, step, 0)


def grid_kernel(window_ref, live_ref, coef_ref, pos_ref, data_ref,
                inner_ref, own_ref, up_ref, down_ref, acc_ref):
    def clear(k, carry):
        for h in range(2):
            acc_ref[h, k] = jnp.zeros(acc_ref.shape[2:], jnp.float32)
        return carry

    lax.fori_loop(0, acc_ref.shape[1], clear, 0)
    grid_slots(window_ref, live_ref, coef_ref, pos_ref, data_ref, acc_ref)

    def fold(row, carry):
        for h in range(2):
            acc_ref[h, row, 0:WIN_COLS, :] += acc_ref[h, row, PLANE:PAD, :]
        return carry

    lax.fori_loop(0, acc_ref.shape[1], fold, 0)

    def put(out_ref, k, row):
        for h in range(2):
            out_ref[k, :, h * LANES : (h + 1) * LANES] = acc_ref[h, row, 0:PLANE, :].astype(out_ref.dtype)

    def put_dense(c, carry):
        for out_ref, first in ((up_ref, 0), (down_ref, TILE_ROWS + 2)):
            for k in range(2):
                pieces = [
                    acc_ref[h, first + k, pl.ds(pl.multiple_of(q * QUARTER + c * WIN_COLS, WIN_COLS), WIN_COLS), :]
                    for q in range(4) for h in range(2)
                ]
                at = pl.ds(pl.multiple_of(c * WIN_COLS, WIN_COLS), WIN_COLS)
                out_ref[k, at, :] = jnp.concatenate(interleave(pieces), axis=1).astype(jnp.bfloat16)
        return carry

    lax.fori_loop(0, QUARTER // WIN_COLS, put_dense, 0)
    for k in range(2):
        put(own_ref, k, 2 + k)
        put(own_ref, 2 + k, TILE_ROWS + k)

    def emit(k, carry):
        put(inner_ref, k, k + 4)
        return carry

    lax.fori_loop(0, TILE_ROWS - 4, emit, 0)


def grid_tile(window, live, coef, pos, data):
    wide = 2 * LANES
    return pl.pallas_call(
        grid_kernel,
        out_shape=[
            jax.ShapeDtypeStruct((TILE_ROWS - 4, PLANE, wide), jnp.bfloat16),
            jax.ShapeDtypeStruct((4, PLANE, wide), jnp.float32),
            jax.ShapeDtypeStruct((2, QUARTER, PLANE), jnp.bfloat16),
            jax.ShapeDtypeStruct((2, QUARTER, PLANE), jnp.bfloat16),
        ],
        in_specs=[SMEM] * 3 + [VMEM] * 2,
        out_specs=[VMEM] * 4,
        scratch_shapes=[pltpu.VMEM((2, TILE_ROWS + 4, PAD, LANES), jnp.float32)],
        compiler_params=pltpu.CompilerParams(vmem_limit_bytes=40 * MB),
        cost_estimate=pl.CostEstimate(flops=6 * 10**9, bytes_accessed=20 * MB, transcendentals=0),
        name="grid_tile",
    )(window, live, coef, pos, data)


def interleave(pieces):
    lane = lax.broadcasted_iota(jnp.int32, pieces[0].shape, 1)
    p = [pieces[0]] + [pltpu.roll(pieces[k], (HALF * k) % LANES, 1) for k in range(1, 8)]
    return [
        jnp.where(lane < 80, p[0], p[1]),
        jnp.where(lane < 32, p[1], jnp.where(lane < 112, p[2], p[3])),
        jnp.where(lane < 64, p[3], p[4]),
        jnp.where(lane < 16, p[4], jnp.where(lane < 96, p[5], p[6])),
        jnp.where(lane < 48, p[6], p[7]),
    ]


def separate(dense):
    lane = lax.broadcasted_iota(jnp.int32, (dense.shape[0], LANES), 1)
    pieces = []
    for k in range(8):
        tile, start = divmod(HALF * k, LANES)
        piece = dense[:, tile * LANES : (tile + 1) * LANES]
        if start + HALF > LANES:
            piece = jnp.where(lane >= start, piece, dense[:, (tile + 1) * LANES : (tile + 2) * LANES])
        if start:
            piece = pltpu.roll(piece, LANES - start, 1)
        pieces.append(jnp.where(lane < HALF, piece, 0.0))
    return pieces


def mid_kernel(ky_ref, inner_table_ref, edge_table_ref, grid_ref, own_ref, up_ref, down_ref, out_ref,
               send_in, send_ed, recv_in, recv_ed, halo, rot, edge_grid, edge_rot, re_ref, im_ref, edge_kx,
               halo_send, halo_recv, send_sem_in, recv_sem_in, send_sem_ed, recv_sem_ed):
    count = lax.axis_size("tile")
    me = lax.axis_index("tile")
    above = lax.rem(me + count - 1, count)
    below = lax.rem(me + 1, count)
    stages = ky_ref.shape[0]
    inner_rows = TILE_ROWS - 4

    barrier = pltpu.get_barrier_semaphore()

    def greet(k, carry):
        pl.semaphore_signal(
            barrier, inc=1, device_id={"tile": lax.rem(me + k, count)}, device_id_type=pl.DeviceIdType.MESH
        )
        return carry

    lax.fori_loop(1, count, greet, 0)
    pl.semaphore_wait(barrier, count - 1)

    def halo_copy(source, way, peer):
        return pltpu.make_async_remote_copy(
            src_ref=source, dst_ref=halo.at[way], send_sem=halo_send.at[way], recv_sem=halo_recv.at[way],
            device_id={"tile": peer}, device_id_type=pl.DeviceIdType.MESH,
        )

    to_below = halo_copy(down_ref, 0, below)
    to_above = halo_copy(up_ref, 1, above)
    to_below.start()
    to_above.start()

    def turned(plane):
        return jnp.concatenate([-plane[:, LANES:], plane[:, :LANES]], axis=1)

    def turn(k, carry):
        rot[k] = turned(grid_ref[k])
        return carry

    lax.fori_loop(0, inner_rows, turn, 0)

    def rows_of(b, k, plane_ref, turned_ref):
        out = jnp.dot(ky_ref[b, :, :PLANE], plane_ref[k], preferred_element_type=jnp.float32)
        out += jnp.dot(ky_ref[b, :, PLANE:], turned_ref[k], preferred_element_type=jnp.float32)
        at = pl.ds(pl.multiple_of(k * LANES, LANES), LANES)
        re_ref[at, :] = out[:, :LANES]
        im_ref[at, :] = out[:, LANES:]

    def pieces_of(start, size):
        pieces = []
        for j in range(4):
            at = pl.ds(start + j, size, stride=LANES)
            pieces += [re_ref[at, :], im_ref[at, :]]
        return jnp.concatenate(interleave(pieces), axis=1)

    def send_all(b, send, recv, send_sem, recv_sem):
        recv[b, me] = send[b, me]

        def to_peer(k, carry):
            peer = lax.rem(me + k, count)
            pltpu.make_async_remote_copy(
                src_ref=send.at[b, peer], dst_ref=recv.at[b, me],
                send_sem=send_sem.at[b], recv_sem=recv_sem.at[b],
                device_id={"tile": peer}, device_id_type=pl.DeviceIdType.MESH,
            ).start()
            return carry

        lax.fori_loop(1, count, to_peer, 0)

    def stage(b, carry):
        def inner_row(k, carry):
            rows_of(b, k, grid_ref, rot)
            return carry

        lax.fori_loop(0, inner_rows, inner_row, 0, unroll=4)

        def inner_pack(d, carry):
            halves = [pieces_of(g * 8 * LANES + d * 4, 8) for g in range(2)]
            send_in[b, d] = jnp.concatenate(halves, axis=0).astype(jnp.bfloat16)
            return carry

        lax.fori_loop(0, count, inner_pack, 0, unroll=4)
        send_all(b, send_in, recv_in, send_sem_in, recv_sem_in)

        @pl.when(b == 0)
        def _():
            to_below.wait()
            to_above.wait()

            def add_halo(c, carry):
                for k in range(4):
                    at = pl.ds(pl.multiple_of(c * WIN_COLS, WIN_COLS), WIN_COLS)
                    pieces = separate(halo[k // 2, k % 2, at, :].astype(jnp.float32))
                    for p, piece in enumerate(pieces):
                        cols = pl.ds(pl.multiple_of(p // 2 * QUARTER + c * WIN_COLS, WIN_COLS), WIN_COLS)
                        lanes = slice(p % 2 * LANES, (p % 2 + 1) * LANES)
                        edge_grid[k, cols, lanes] = (own_ref[k, cols, lanes] + piece).astype(jnp.bfloat16)
                return carry

            lax.fori_loop(0, QUARTER // WIN_COLS, add_halo, 0)
            for k in range(4):
                edge_rot[k] = turned(edge_grid[k])

        def edge_row(k, carry):
            rows_of(b, k, edge_grid, edge_rot)
            return carry

        lax.fori_loop(0, 4, edge_row, 0, unroll=4)

        def edge_pack(d, carry):
            send_ed[b, d] = pieces_of(d * 4, 4).astype(jnp.bfloat16)
            return carry

        lax.fori_loop(0, count, edge_pack, 0, unroll=4)
        send_all(b, send_ed, recv_ed, send_sem_ed, recv_sem_ed)
        return carry

    lax.fori_loop(0, stages, stage, 0)

    lane = lax.rem(lax.broadcasted_iota(jnp.int32, (320, PLANE), 1), 2 * HALF)
    real = lane < HALF

    def others(b, ref, send_sem, recv_sem):
        return pltpu.make_async_remote_copy(
            src_ref=ref.at[b, pl.ds(0, count - 1)], dst_ref=ref.at[b, pl.ds(0, count - 1)],
            send_sem=send_sem.at[b], recv_sem=recv_sem.at[b],
            device_id={"tile": below}, device_id_type=pl.DeviceIdType.MESH,
        )

    def finish(b, carry):
        others(b, recv_in, send_sem_in, recv_sem_in).wait_recv()
        others(b, recv_ed, send_sem_ed, recv_sem_ed).wait_recv()

        def lift(s, carry):
            pair = [recv_ed[b, 2 * s + k].astype(jnp.float32) for k in range(2)]
            edge_kx[pl.ds(pl.multiple_of(8 * s, 8), 8), :] = jnp.concatenate(pair, axis=0)
            return carry

        lax.fori_loop(0, count // 2, lift, 0)
        inner = recv_in[b].reshape(count * inner_rows, PLANE)
        edge = edge_kx[...].astype(jnp.bfloat16)
        for h in range(2):
            rows = slice(320 * h, 320 * (h + 1))

            def product(part):
                return jnp.dot(
                    inner_table_ref[part, rows, :], inner, preferred_element_type=jnp.float32
                ) + jnp.dot(edge_table_ref[part, rows, :], edge, preferred_element_type=jnp.float32)

            first = product(0)
            second = product(1)
            ahead = pltpu.roll(second, PLANE - HALF, 1)
            behind = pltpu.roll(second, HALF, 1)
            out = first + jnp.where(real, -ahead, behind)
            at = pl.ds(pl.multiple_of(b * PLANE, PLANE), PLANE)
            out_ref[rows, at] = (out * (1.0 / PLANE)).astype(jnp.bfloat16)
        return carry

    lax.fori_loop(0, stages, finish, 0)

    def sent(b, carry):
        others(b, send_in, send_sem_in, recv_sem_in).wait_send()
        others(b, send_ed, send_sem_ed, recv_sem_ed).wait_send()
        return carry

    lax.fori_loop(0, stages, sent, 0)


def transform_plane(ky_table, inner_table, edge_table, grid, own, up, down):
    stages, count, rows, wide = 5, 32, TILE_ROWS - 4, 2 * LANES
    bf16, f32 = jnp.bfloat16, jnp.float32
    dma = pltpu.SemaphoreType.DMA
    return pl.pallas_call(
        mid_kernel,
        out_shape=jax.ShapeDtypeStruct((PLANE, stages * PLANE), bf16),
        in_specs=[VMEM] * 7,
        out_specs=VMEM,
        scratch_shapes=[
            pltpu.VMEM((stages, count, rows, PLANE), bf16),
            pltpu.VMEM((stages, count, 4, PLANE), bf16),
            pltpu.VMEM((stages, count, rows, PLANE), bf16),
            pltpu.VMEM((stages, count, 4, PLANE), bf16),
            pltpu.VMEM((2, 2, QUARTER, PLANE), bf16),
            pltpu.VMEM((rows, PLANE, wide), bf16),
            pltpu.VMEM((4, PLANE, wide), bf16),
            pltpu.VMEM((4, PLANE, wide), bf16),
            pltpu.VMEM((rows * LANES, LANES), f32),
            pltpu.VMEM((rows * LANES, LANES), f32),
            pltpu.VMEM((4 * count, PLANE), f32),
            dma((2,)), dma((2,)), dma((stages,)), dma((stages,)), dma((stages,)), dma((stages,)),
        ],
        compiler_params=pltpu.CompilerParams(
            vmem_limit_bytes=36 * MB, collective_id=0, has_side_effects=True
        ),
        cost_estimate=pl.CostEstimate(flops=20 * 10**9, bytes_accessed=20 * MB, transcendentals=0),
        name="plane",
    )(ky_table, inner_table, edge_table, grid, own, up, down)


def make_tables():
    idx = np.arange(PLANE)
    phase = (idx[:, None] * idx[None, :] % PLANE).astype(np.float32) * np.float32(2.0 * math.pi / PLANE)
    cos_tab = np.cos(phase).astype(ml_dtypes.bfloat16)
    sin_tab = np.sin(phase).astype(ml_dtypes.bfloat16)
    ky_table = np.concatenate([cos_tab, sin_tab], axis=1)
    ky_table = ky_table.reshape(32, 5, 4, 2 * PLANE).transpose(1, 0, 2, 3).reshape(5, LANES, 2 * PLANE)
    both = np.stack([cos_tab, sin_tab]).reshape(2, PLANE, 32, TILE_ROWS)
    inner_table = both[..., 2:18].reshape(2, PLANE, 512)
    edge_table = np.concatenate([both[..., 0:2], both[..., 18:20]], axis=-1).reshape(2, PLANE, 128)
    return ky_table, inner_table, edge_table


def body(coil_data, frame_of, basis, sample_pos, window_at, live_count):
    parts, tiles, slots, pair, samples = coil_data.shape[2:]
    devices = parts * tiles
    frames = frame_of[0, 0].transpose(0, 2, 1)
    table = jnp.concatenate([basis, basis], axis=1).astype(jnp.float32)
    data, coef = exchange(frames, table, coil_data.reshape(devices, slots * pair, samples))
    window = window_at[0, 0].transpose(0, 2, 3, 1)
    pos = sample_pos.reshape(devices * slots, 2, samples)
    inner, own, up, down = grid_tile(window, live_count[0, 0], coef, pos, data)
    ky_table, inner_table, edge_table = [jnp.asarray(t) for t in make_tables()]
    return transform_plane(ky_table, inner_table, edge_table, inner, own, up, down)[None]


def solution(mesh):
    return jax.shard_map(
        body,
        mesh=mesh,
        in_specs=(
            P("kz", "tile", None, None, None, None, None),
            P("kz", "tile", None, None, None),
            P(),
            P("kz", "tile", None, None, None, None, None),
            P("kz", "tile", None, None, None, None),
            P("kz", "tile", None, None),
        ),
        out_specs=P("kz", None, "tile"),
        check_vma=False,
    )
```

```python
import functools
import math

import jax
import jax.numpy as jnp
from jax import lax
from jax.experimental import pallas as pl
from jax.experimental.pallas import tpu as pltpu
from jax.sharding import PartitionSpec as P
import ml_dtypes
import numpy as np

PLANE = 640
WIN_ROWS = 4
WIN_COLS = 32
TILE_ROWS = 20
PAD = PLANE + WIN_COLS
LANES = 128
HALF = 80
QUARTER = PLANE // 4
RANK = 10
DEPTH = 8
MB = 1024 * 1024


def taper(dist):
    inner = 1.0 - (dist * (1.0 / 1.5)) * (dist * (1.0 / 1.5))
    inner = jnp.maximum(inner, 0.0)
    return inner * inner


SMEM = pl.BlockSpec(memory_space=pltpu.SMEM)
VMEM = pl.BlockSpec(memory_space=pltpu.VMEM)
HBM = pl.BlockSpec(memory_space=pltpu.HBM)


def exchange_kernel(frame_ref, data_ref, data_out, frame_out, spread, met, total,
                    ready, data_send, data_recv, met_send, met_recv, frame_send, frame_recv, own_sem):
    parts, tiles = lax.axis_size("kz"), lax.axis_size("tile")
    kz, tile = lax.axis_index("kz"), lax.axis_index("tile")
    devices = parts * tiles
    me = kz * tiles + tile
    barrier = pltpu.get_barrier_semaphore()

    def signal(sem, part, spot):
        pl.semaphore_signal(sem, inc=1, device_id=(part, spot), device_id_type=pl.DeviceIdType.MESH)

    def greet_tile(k, carry):
        signal(barrier, kz, lax.rem(tile + k, tiles))
        return carry

    def greet_part(k, carry):
        signal(barrier, lax.rem(kz + k, parts), tile)
        return carry

    def tell_part(k, carry):
        signal(ready, lax.rem(kz + k, parts), tile)
        return carry

    lax.fori_loop(1, tiles, greet_tile, 0)
    lax.fori_loop(1, parts, greet_part, 0)
    pl.semaphore_wait(barrier, tiles + parts - 2)
    lax.fori_loop(1, parts, tell_part, 0)
    pl.semaphore_wait(ready, parts - 1)

    def copy_to(part, spot, src, dst, send, recv):
        return pltpu.make_async_remote_copy(
            src_ref=src, dst_ref=dst, send_sem=send, recv_sem=recv,
            device_id=(part, spot), device_id_type=pl.DeviceIdType.MESH,
        )

    def send_data(k, carry):
        part = lax.rem(kz + k // tiles, parts)
        spot = lax.rem(tile + lax.rem(k, tiles), tiles)
        to = part * tiles + spot
        copy_to(part, spot, data_ref.at[to], data_out.at[me], data_send, data_recv).start()
        return carry

    lax.fori_loop(1, tiles, send_data, 0)

    columns = tiles // DEPTH
    groups = parts * columns
    column, level = tile // DEPTH, lax.rem(tile, DEPTH)
    mine = kz * columns + column
    lane = lax.broadcasted_iota(jnp.int32, (1, LANES), 1)

    def place(d, carry):
        first, second = [frame_ref[d // tiles, s, lax.rem(d, tiles)] for s in range(2)]
        spread[d] = jnp.where(lane == 2 * mine, first, jnp.where(lane == 2 * mine + 1, second, 0))
        return carry

    lax.fori_loop(0, devices, place, 0, unroll=8)

    def send_met(k, carry):
        group = lax.rem(mine + k, groups)
        part, spot = group // columns, lax.rem(group, columns) * DEPTH + level
        levels = pl.ds(group * DEPTH, DEPTH)
        copy_to(part, spot, spread.at[levels], met.at[mine], met_send, met_recv).start()
        return carry

    lax.fori_loop(1, groups, send_met, 0)
    lax.fori_loop(tiles, devices, send_data, 0)
    own = pltpu.make_async_copy(data_ref.at[me], data_out.at[me], own_sem)
    own.start()
    met[mine] = spread[pl.ds(mine * DEPTH, DEPTH)]
    others = pl.ds(0, groups - 1)
    rows = pl.ds(0, (groups - 1) * DEPTH)
    copy_to(kz, lax.rem(tile + 1, tiles), spread.at[rows], spread.at[rows], met_send, met_recv).wait_send()
    copy_to(kz, lax.rem(tile + 1, tiles), met.at[others], met.at[others], met_send, met_recv).wait_recv()

    def add(g, carry):
        return carry + met[g]

    total[...] = lax.fori_loop(0, groups, add, jnp.zeros(total.shape, jnp.int32))

    def send_frames(k, carry):
        to = lax.rem(level + k, DEPTH)
        copy_to(kz, column * DEPTH + to, total.at[to], frame_out.at[level], frame_send, frame_recv).start()
        return carry

    lax.fori_loop(1, DEPTH, send_frames, 0)
    frame_out[level] = total[level]
    own.wait()
    others = pl.ds(0, devices - 1)
    levels = pl.ds(0, DEPTH - 1)
    beside = (kz, lax.rem(tile + 1, tiles))
    for every in (
        copy_to(*beside, data_ref.at[others], data_out.at[others], data_send, data_recv),
        copy_to(*beside, total.at[levels], frame_out.at[levels], frame_send, frame_recv),
    ):
        every.wait_send()
        every.wait_recv()


def exchange(frames, data):
    dma = pltpu.SemaphoreType.DMA
    devices = data.shape[0]
    groups = devices // DEPTH
    return pl.pallas_call(
        exchange_kernel,
        out_shape=[
            jax.ShapeDtypeStruct(data.shape, data.dtype),
            jax.ShapeDtypeStruct((DEPTH, 1, LANES), jnp.int32),
        ],
        in_specs=[SMEM, HBM],
        out_specs=[VMEM, VMEM],
        scratch_shapes=[
            pltpu.VMEM((devices, 1, LANES), jnp.int32),
            pltpu.VMEM((groups, DEPTH, 1, LANES), jnp.int32),
            pltpu.VMEM((DEPTH, 1, LANES), jnp.int32),
            pltpu.SemaphoreType.REGULAR,
        ] + [dma] * 7,
        compiler_params=pltpu.CompilerParams(collective_id=1, has_side_effects=True, vmem_limit_bytes=50 * MB),
        cost_estimate=pl.CostEstimate(flops=0, bytes_accessed=4 * MB, transcendentals=0),
        name="exchange",
    )(frames, data)


def grid_slots(window_ref, live_ref, frame_ref, basis_ref, pos_ref, data_ref, acc_ref):
    parts, slots, _, tiles = window_ref.shape
    row_cell = lax.broadcasted_iota(jnp.int32, (8, LANES), 0).astype(jnp.float32)
    col_cell = lax.broadcasted_iota(jnp.int32, (WIN_COLS, LANES), 0).astype(jnp.float32)
    zero = jnp.zeros((LANES - HALF, LANES), jnp.bfloat16)

    def contribution(a, t, s):
        pair = a * tiles + t
        place = pos_ref[pair * slots + s]
        living = (s < live_ref[a, t]).astype(jnp.float32)
        row_k = taper(row_cell - place[0:1, :]) * living
        col_k = taper(col_cell - place[1:2, :])
        weight = jnp.concatenate([row_k[i : i + 1, :] * col_k for i in range(WIN_ROWS)], axis=0)
        weight = weight.astype(jnp.bfloat16)
        data = data_ref[pair, 16 * s : 16 * (s + 1)].astype(jnp.float32)
        frame = frame_ref[t % DEPTH, 0, 2 * (a * (tiles // DEPTH) + t // DEPTH) + s]
        scale = [basis_ref[r, frame] for r in range(RANK)]
        across = (((1,), (1,)), ((), ()))
        halves = []
        for half in (data[0:8], data[8:16]):
            values = jnp.concatenate([half * c for c in scale], axis=0).astype(jnp.bfloat16)
            values = jnp.concatenate([values, zero], axis=0)
            halves.append(lax.dot_general(weight, values, across, preferred_element_type=jnp.float32))
        return halves

    def step(a, carry):
        slot_ids = [(t, s) for t in range(tiles) for s in range(slots)]
        sums = [contribution(a, t, s) for t, s in slot_ids]
        for (t, s), halves in zip(slot_ids, sums):
            row = window_ref[a, s, 0, t] + 2
            col = window_ref[a, s, 1, t]
            for i in range(WIN_ROWS):
                for h, half in enumerate(halves):
                    at = (h, row + i, pl.ds(col, WIN_COLS), slice(None))
                    acc_ref[at] += half[i * WIN_COLS : (i + 1) * WIN_COLS]
        return carry

    lax.fori_loop(0, parts, step, 0)


def grid_kernel(window_ref, live_ref, frame_ref, basis_ref, pos_ref, data_ref,
                inner_ref, own_ref, up_ref, down_ref, acc_ref):
    def clear(k, carry):
        for h in range(2):
            acc_ref[h, k] = jnp.zeros(acc_ref.shape[2:], jnp.float32)
        return carry

    lax.fori_loop(0, acc_ref.shape[1], clear, 0)
    grid_slots(window_ref, live_ref, frame_ref, basis_ref, pos_ref, data_ref, acc_ref)

    def fold(row, carry):
        for h in range(2):
            acc_ref[h, row, 0:WIN_COLS, :] += acc_ref[h, row, PLANE:PAD, :]
        return carry

    lax.fori_loop(0, acc_ref.shape[1], fold, 0)

    def put(out_ref, k, row):
        for h in range(2):
            out_ref[k, :, h * LANES : (h + 1) * LANES] = acc_ref[h, row, 0:PLANE, :].astype(out_ref.dtype)

    def put_dense(c, carry):
        for out_ref, first in ((up_ref, 0), (down_ref, TILE_ROWS + 2)):
            for k in range(2):
                pieces = [
                    acc_ref[h, first + k, pl.ds(pl.multiple_of(q * QUARTER + c * WIN_COLS, WIN_COLS), WIN_COLS), :]
                    for q in range(4) for h in range(2)
                ]
                at = pl.ds(pl.multiple_of(c * WIN_COLS, WIN_COLS), WIN_COLS)
                out_ref[k, at, :] = jnp.concatenate(interleave(pieces), axis=1).astype(jnp.bfloat16)
        return carry

    lax.fori_loop(0, QUARTER // WIN_COLS, put_dense, 0)
    for k in range(2):
        put(own_ref, k, 2 + k)
        put(own_ref, 2 + k, TILE_ROWS + k)

    def emit(k, carry):
        put(inner_ref, k, k + 4)
        return carry

    lax.fori_loop(0, TILE_ROWS - 4, emit, 0)


def grid_tile(window, live, frames, basis, pos, data):
    wide = 2 * LANES
    return pl.pallas_call(
        grid_kernel,
        out_shape=[
            jax.ShapeDtypeStruct((TILE_ROWS - 4, PLANE, wide), jnp.bfloat16),
            jax.ShapeDtypeStruct((4, PLANE, wide), jnp.float32),
            jax.ShapeDtypeStruct((2, QUARTER, PLANE), jnp.bfloat16),
            jax.ShapeDtypeStruct((2, QUARTER, PLANE), jnp.bfloat16),
        ],
        in_specs=[SMEM] * 4 + [VMEM] * 2,
        out_specs=[VMEM] * 4,
        scratch_shapes=[pltpu.VMEM((2, TILE_ROWS + 4, PAD, LANES), jnp.float32)],
        compiler_params=pltpu.CompilerParams(vmem_limit_bytes=40 * MB),
        cost_estimate=pl.CostEstimate(flops=6 * 10**9, bytes_accessed=20 * MB, transcendentals=0),
        name="grid_tile",
    )(window, live, frames, basis, pos, data)


def interleave(pieces):
    lane = lax.broadcasted_iota(jnp.int32, pieces[0].shape, 1)
    p = [pieces[0]] + [pltpu.roll(pieces[k], (HALF * k) % LANES, 1) for k in range(1, 8)]
    return [
        jnp.where(lane < 80, p[0], p[1]),
        jnp.where(lane < 32, p[1], jnp.where(lane < 112, p[2], p[3])),
        jnp.where(lane < 64, p[3], p[4]),
        jnp.where(lane < 16, p[4], jnp.where(lane < 96, p[5], p[6])),
        jnp.where(lane < 48, p[6], p[7]),
    ]


def separate(dense):
    lane = lax.broadcasted_iota(jnp.int32, (dense.shape[0], LANES), 1)
    pieces = []
    for k in range(8):
        tile, start = divmod(HALF * k, LANES)
        piece = dense[:, tile * LANES : (tile + 1) * LANES]
        if start + HALF > LANES:
            piece = jnp.where(lane >= start, piece, dense[:, (tile + 1) * LANES : (tile + 2) * LANES])
        if start:
            piece = pltpu.roll(piece, LANES - start, 1)
        pieces.append(jnp.where(lane < HALF, piece, 0.0))
    return pieces


def mid_kernel(ky_ref, inner_table_ref, edge_table_ref, grid_ref, own_ref, up_ref, down_ref, out_ref,
               send_in, send_ed, recv_in, recv_ed, halo, rot, edge_grid, edge_rot, re_ref, im_ref, edge_kx,
               halo_send, halo_recv, send_sem_in, recv_sem_in, send_sem_ed, recv_sem_ed):
    count = lax.axis_size("tile")
    me = lax.axis_index("tile")
    above = lax.rem(me + count - 1, count)
    below = lax.rem(me + 1, count)
    stages = ky_ref.shape[0]
    inner_rows = TILE_ROWS - 4

    barrier = pltpu.get_barrier_semaphore()

    def greet(k, carry):
        pl.semaphore_signal(
            barrier, inc=1, device_id={"tile": lax.rem(me + k, count)}, device_id_type=pl.DeviceIdType.MESH
        )
        return carry

    lax.fori_loop(1, count, greet, 0)
    pl.semaphore_wait(barrier, count - 1)

    def halo_copy(source, way, peer):
        return pltpu.make_async_remote_copy(
            src_ref=source, dst_ref=halo.at[way], send_sem=halo_send.at[way], recv_sem=halo_recv.at[way],
            device_id={"tile": peer}, device_id_type=pl.DeviceIdType.MESH,
        )

    to_below = halo_copy(down_ref, 0, below)
    to_above = halo_copy(up_ref, 1, above)
    to_below.start()
    to_above.start()

    def turned(plane):
        return jnp.concatenate([-plane[:, LANES:], plane[:, :LANES]], axis=1)

    def turn(k, carry):
        rot[k] = turned(grid_ref[k])
        return carry

    lax.fori_loop(0, inner_rows, turn, 0)

    def rows_of(b, k, plane_ref, turned_ref):
        out = jnp.dot(ky_ref[b, :, :PLANE], plane_ref[k], preferred_element_type=jnp.float32)
        out += jnp.dot(ky_ref[b, :, PLANE:], turned_ref[k], preferred_element_type=jnp.float32)
        at = pl.ds(pl.multiple_of(k * LANES, LANES), LANES)
        re_ref[at, :] = out[:, :LANES]
        im_ref[at, :] = out[:, LANES:]

    def pieces_of(start, size):
        pieces = []
        for j in range(4):
            at = pl.ds(start + j, size, stride=LANES)
            pieces += [re_ref[at, :], im_ref[at, :]]
        return jnp.concatenate(interleave(pieces), axis=1)

    def send_all(b, send, recv, send_sem, recv_sem):
        recv[b, me] = send[b, me]

        def to_peer(k, carry):
            peer = lax.rem(me + k, count)
            pltpu.make_async_remote_copy(
                src_ref=send.at[b, peer], dst_ref=recv.at[b, me],
                send_sem=send_sem.at[b], recv_sem=recv_sem.at[b],
                device_id={"tile": peer}, device_id_type=pl.DeviceIdType.MESH,
            ).start()
            return carry

        lax.fori_loop(1, count, to_peer, 0)

    def stage(b, carry):
        def inner_row(k, carry):
            rows_of(b, k, grid_ref, rot)
            return carry

        lax.fori_loop(0, inner_rows, inner_row, 0, unroll=4)

        def inner_pack(d, carry):
            halves = [pieces_of(g * 8 * LANES + d * 4, 8) for g in range(2)]
            send_in[b, d] = jnp.concatenate(halves, axis=0).astype(jnp.bfloat16)
            return carry

        lax.fori_loop(0, count, inner_pack, 0, unroll=4)
        send_all(b, send_in, recv_in, send_sem_in, recv_sem_in)

        @pl.when(b == 0)
        def _():
            to_below.wait()
            to_above.wait()

            def add_halo(c, carry):
                for k in range(4):
                    at = pl.ds(pl.multiple_of(c * WIN_COLS, WIN_COLS), WIN_COLS)
                    pieces = separate(halo[k // 2, k % 2, at, :].astype(jnp.float32))
                    for p, piece in enumerate(pieces):
                        cols = pl.ds(pl.multiple_of(p // 2 * QUARTER + c * WIN_COLS, WIN_COLS), WIN_COLS)
                        lanes = slice(p % 2 * LANES, (p % 2 + 1) * LANES)
                        edge_grid[k, cols, lanes] = (own_ref[k, cols, lanes] + piece).astype(jnp.bfloat16)
                return carry

            lax.fori_loop(0, QUARTER // WIN_COLS, add_halo, 0)
            for k in range(4):
                edge_rot[k] = turned(edge_grid[k])

        def edge_row(k, carry):
            rows_of(b, k, edge_grid, edge_rot)
            return carry

        lax.fori_loop(0, 4, edge_row, 0, unroll=4)

        def edge_pack(d, carry):
            send_ed[b, d] = pieces_of(d * 4, 4).astype(jnp.bfloat16)
            return carry

        lax.fori_loop(0, count, edge_pack, 0, unroll=4)
        send_all(b, send_ed, recv_ed, send_sem_ed, recv_sem_ed)
        return carry

    lax.fori_loop(0, stages, stage, 0)

    lane = lax.rem(lax.broadcasted_iota(jnp.int32, (320, PLANE), 1), 2 * HALF)
    real = lane < HALF

    def others(b, ref, send_sem, recv_sem):
        return pltpu.make_async_remote_copy(
            src_ref=ref.at[b, pl.ds(0, count - 1)], dst_ref=ref.at[b, pl.ds(0, count - 1)],
            send_sem=send_sem.at[b], recv_sem=recv_sem.at[b],
            device_id={"tile": below}, device_id_type=pl.DeviceIdType.MESH,
        )

    def finish(b, carry):
        others(b, recv_in, send_sem_in, recv_sem_in).wait_recv()
        others(b, recv_ed, send_sem_ed, recv_sem_ed).wait_recv()

        def lift(s, carry):
            pair = [recv_ed[b, 2 * s + k].astype(jnp.float32) for k in range(2)]
            edge_kx[pl.ds(pl.multiple_of(8 * s, 8), 8), :] = jnp.concatenate(pair, axis=0)
            return carry

        lax.fori_loop(0, count // 2, lift, 0)
        inner = recv_in[b].reshape(count * inner_rows, PLANE)
        edge = edge_kx[...].astype(jnp.bfloat16)
        for h in range(2):
            rows = slice(320 * h, 320 * (h + 1))

            def product(part):
                return jnp.dot(
                    inner_table_ref[part, rows, :], inner, preferred_element_type=jnp.float32
                ) + jnp.dot(edge_table_ref[part, rows, :], edge, preferred_element_type=jnp.float32)

            first = product(0)
            second = product(1)
            ahead = pltpu.roll(second, PLANE - HALF, 1)
            behind = pltpu.roll(second, HALF, 1)
            out = first + jnp.where(real, -ahead, behind)
            at = pl.ds(pl.multiple_of(b * PLANE, PLANE), PLANE)
            out_ref[rows, at] = (out * (1.0 / PLANE)).astype(jnp.bfloat16)
        return carry

    lax.fori_loop(0, stages, finish, 0)

    def sent(b, carry):
        others(b, send_in, send_sem_in, recv_sem_in).wait_send()
        others(b, send_ed, send_sem_ed, recv_sem_ed).wait_send()
        return carry

    lax.fori_loop(0, stages, sent, 0)


def transform_plane(ky_table, inner_table, edge_table, grid, own, up, down):
    stages, count, rows, wide = 5, 32, TILE_ROWS - 4, 2 * LANES
    bf16, f32 = jnp.bfloat16, jnp.float32
    dma = pltpu.SemaphoreType.DMA
    return pl.pallas_call(
        mid_kernel,
        out_shape=jax.ShapeDtypeStruct((PLANE, stages * PLANE), bf16),
        in_specs=[VMEM] * 7,
        out_specs=VMEM,
        scratch_shapes=[
            pltpu.VMEM((stages, count, rows, PLANE), bf16),
            pltpu.VMEM((stages, count, 4, PLANE), bf16),
            pltpu.VMEM((stages, count, rows, PLANE), bf16),
            pltpu.VMEM((stages, count, 4, PLANE), bf16),
            pltpu.VMEM((2, 2, QUARTER, PLANE), bf16),
            pltpu.VMEM((rows, PLANE, wide), bf16),
            pltpu.VMEM((4, PLANE, wide), bf16),
            pltpu.VMEM((4, PLANE, wide), bf16),
            pltpu.VMEM((rows * LANES, LANES), f32),
            pltpu.VMEM((rows * LANES, LANES), f32),
            pltpu.VMEM((4 * count, PLANE), f32),
            dma((2,)), dma((2,)), dma((stages,)), dma((stages,)), dma((stages,)), dma((stages,)),
        ],
        compiler_params=pltpu.CompilerParams(
            vmem_limit_bytes=36 * MB, collective_id=0, has_side_effects=True
        ),
        cost_estimate=pl.CostEstimate(flops=20 * 10**9, bytes_accessed=20 * MB, transcendentals=0),
        name="plane",
    )(ky_table, inner_table, edge_table, grid, own, up, down)


def make_tables():
    idx = np.arange(PLANE)
    phase = (idx[:, None] * idx[None, :] % PLANE).astype(np.float32) * np.float32(2.0 * math.pi / PLANE)
    cos_tab = np.cos(phase).astype(ml_dtypes.bfloat16)
    sin_tab = np.sin(phase).astype(ml_dtypes.bfloat16)
    ky_table = np.concatenate([cos_tab, sin_tab], axis=1)
    ky_table = ky_table.reshape(32, 5, 4, 2 * PLANE).transpose(1, 0, 2, 3).reshape(5, LANES, 2 * PLANE)
    both = np.stack([cos_tab, sin_tab]).reshape(2, PLANE, 32, TILE_ROWS)
    inner_table = both[..., 2:18].reshape(2, PLANE, 512)
    edge_table = np.concatenate([both[..., 0:2], both[..., 18:20]], axis=-1).reshape(2, PLANE, 128)
    return ky_table, inner_table, edge_table


def body(coil_data, frame_of, basis, sample_pos, window_at, live_count):
    parts, tiles, slots, pair, samples = coil_data.shape[2:]
    devices = parts * tiles
    frames = frame_of[0, 0].transpose(0, 2, 1)
    table = basis.T.astype(jnp.float32)
    data, frames = exchange(frames, coil_data.reshape(devices, slots * pair, samples))
    window = window_at[0, 0].transpose(0, 2, 3, 1)
    pos = sample_pos.reshape(devices * slots, 2, samples)
    inner, own, up, down = grid_tile(window, live_count[0, 0], frames, table, pos, data)
    ky_table, inner_table, edge_table = [jnp.asarray(t) for t in make_tables()]
    return transform_plane(ky_table, inner_table, edge_table, inner, own, up, down)[None]


def solution(mesh):
    return jax.shard_map(
        body,
        mesh=mesh,
        in_specs=(
            P("kz", "tile", None, None, None, None, None),
            P("kz", "tile", None, None, None),
            P(),
            P("kz", "tile", None, None, None, None, None),
            P("kz", "tile", None, None, None, None),
            P("kz", "tile", None, None),
        ),
        out_specs=P("kz", None, "tile"),
        check_vma=False,
    )
```

```python
import functools
import math

import jax
import jax.numpy as jnp
from jax import lax
from jax.experimental import pallas as pl
from jax.experimental.pallas import tpu as pltpu
from jax.sharding import PartitionSpec as P
import ml_dtypes
import numpy as np

PLANE = 640
WIN_ROWS = 4
WIN_COLS = 32
TILE_ROWS = 20
PAD = PLANE + WIN_COLS
LANES = 128
HALF = 80
QUARTER = PLANE // 4
RANK = 10
DEPTH = 8
MB = 1024 * 1024


def taper(dist):
    inner = 1.0 - (dist * (1.0 / 1.5)) * (dist * (1.0 / 1.5))
    inner = jnp.maximum(inner, 0.0)
    return inner * inner


SMEM = pl.BlockSpec(memory_space=pltpu.SMEM)
VMEM = pl.BlockSpec(memory_space=pltpu.VMEM)
HBM = pl.BlockSpec(memory_space=pltpu.HBM)


def exchange_kernel(frame_ref, basis_ref, data_ref, data_out, frame_out, basis_out, sums_out, spread, met, total,
                    ready, data_send, data_recv, met_send, met_recv, frame_send, frame_recv, own_sem):
    parts, tiles = lax.axis_size("kz"), lax.axis_size("tile")
    kz, tile = lax.axis_index("kz"), lax.axis_index("tile")
    devices = parts * tiles
    me = kz * tiles + tile
    barrier = pltpu.get_barrier_semaphore()

    def signal(sem, part, spot):
        pl.semaphore_signal(sem, inc=1, device_id=(part, spot), device_id_type=pl.DeviceIdType.MESH)

    def greet_tile(k, carry):
        signal(barrier, kz, lax.rem(tile + k, tiles))
        return carry

    def greet_part(k, carry):
        signal(barrier, lax.rem(kz + k, parts), tile)
        return carry

    def tell_part(k, carry):
        signal(ready, lax.rem(kz + k, parts), tile)
        return carry

    lax.fori_loop(1, tiles, greet_tile, 0)
    lax.fori_loop(1, parts, greet_part, 0)
    pl.semaphore_wait(barrier, tiles + parts - 2)
    lax.fori_loop(1, parts, tell_part, 0)

    def copy_to(part, spot, src, dst, send, recv):
        return pltpu.make_async_remote_copy(
            src_ref=src, dst_ref=dst, send_sem=send, recv_sem=recv,
            device_id=(part, spot), device_id_type=pl.DeviceIdType.MESH,
        )

    def send_data(k, carry):
        part = lax.rem(kz + k // tiles, parts)
        spot = lax.rem(tile + lax.rem(k, tiles), tiles)
        to = part * tiles + spot
        copy_to(part, spot, data_ref.at[to], data_out.at[me], data_send, data_recv).start()
        return carry

    lax.fori_loop(1, tiles, send_data, 0)

    columns = tiles // DEPTH
    groups = parts * columns
    column, level = tile // DEPTH, lax.rem(tile, DEPTH)
    mine = kz * columns + column
    lane = lax.broadcasted_iota(jnp.int32, (1, LANES), 1)

    def place(d, carry):
        first, second = [frame_ref[d // tiles, s, lax.rem(d, tiles)] for s in range(2)]
        spread[d] = jnp.where(lane == 2 * mine, first, jnp.where(lane == 2 * mine + 1, second, 0))
        return carry

    lax.fori_loop(0, devices, place, 0, unroll=8)

    pl.semaphore_wait(ready, parts - 1)

    def send_met(k, carry):
        group = lax.rem(mine + k, groups)
        part, spot = group // columns, lax.rem(group, columns) * DEPTH + level
        levels = pl.ds(group * DEPTH, DEPTH)
        copy_to(part, spot, spread.at[levels], met.at[mine], met_send, met_recv).start()
        return carry

    lax.fori_loop(1, groups, send_met, 0)
    lax.fori_loop(tiles, devices, send_data, 0)
    own = pltpu.make_async_copy(data_ref.at[me], data_out.at[me], own_sem)
    own.start()
    met[mine] = spread[pl.ds(mine * DEPTH, DEPTH)]
    basis_out[...] = basis_ref[...].astype(jnp.float32)
    others = pl.ds(0, groups - 1)
    rows = pl.ds(0, (groups - 1) * DEPTH)
    copy_to(kz, lax.rem(tile + 1, tiles), spread.at[rows], spread.at[rows], met_send, met_recv).wait_send()
    copy_to(kz, lax.rem(tile + 1, tiles), met.at[others], met.at[others], met_send, met_recv).wait_recv()

    def add(g, carry):
        return carry + met[g]

    total[...] = lax.fori_loop(0, groups, add, jnp.zeros(total.shape, jnp.int32))

    def send_frames(k, carry):
        to = lax.rem(level + k, DEPTH)
        copy_to(kz, column * DEPTH + to, total.at[to], frame_out.at[level], frame_send, frame_recv).start()
        return carry

    lax.fori_loop(1, DEPTH, send_frames, 0)
    frame_out[level] = total[level]

    def clear(k, carry):
        for h in range(2):
            sums_out[h, k] = jnp.zeros(sums_out.shape[2:], jnp.float32)
        return carry

    lax.fori_loop(0, sums_out.shape[1], clear, 0)
    own.wait()
    others = pl.ds(0, devices - 1)
    levels = pl.ds(0, DEPTH - 1)
    beside = (kz, lax.rem(tile + 1, tiles))
    for every in (
        copy_to(*beside, data_ref.at[others], data_out.at[others], data_send, data_recv),
        copy_to(*beside, total.at[levels], frame_out.at[levels], frame_send, frame_recv),
    ):
        every.wait_send()
        every.wait_recv()


def exchange(frames, basis, data):
    dma = pltpu.SemaphoreType.DMA
    devices = data.shape[0]
    groups = devices // DEPTH
    return pl.pallas_call(
        exchange_kernel,
        out_shape=[
            jax.ShapeDtypeStruct(data.shape, data.dtype),
            jax.ShapeDtypeStruct((DEPTH, 1, LANES), jnp.int32),
            jax.ShapeDtypeStruct(basis.shape, jnp.float32),
            jax.ShapeDtypeStruct((2, TILE_ROWS + 4, PAD, LANES), jnp.float32),
        ],
        in_specs=[SMEM, VMEM, HBM],
        out_specs=[VMEM] * 4,
        scratch_shapes=[
            pltpu.VMEM((devices, 1, LANES), jnp.int32),
            pltpu.VMEM((groups, DEPTH, 1, LANES), jnp.int32),
            pltpu.VMEM((DEPTH, 1, LANES), jnp.int32),
            pltpu.SemaphoreType.REGULAR,
        ] + [dma] * 7,
        compiler_params=pltpu.CompilerParams(collective_id=1, has_side_effects=True, vmem_limit_bytes=8 * MB),
        cost_estimate=pl.CostEstimate(flops=6 * 10**10, bytes_accessed=4 * MB, transcendentals=0),
        name="exchange",
    )(frames, basis, data)


def grid_slots(window_ref, live_ref, frame_ref, basis_ref, pos_ref, data_ref, acc_ref):
    parts, slots, _, tiles = window_ref.shape
    row_cell = lax.broadcasted_iota(jnp.int32, (8, LANES), 0).astype(jnp.float32)
    col_cell = lax.broadcasted_iota(jnp.int32, (WIN_COLS, LANES), 0).astype(jnp.float32)
    zero = jnp.zeros((LANES - HALF, LANES), jnp.bfloat16)

    def contribution(a, t, s):
        pair = a * tiles + t
        place = pos_ref[pair * slots + s]
        living = (s < live_ref[a, t]).astype(jnp.float32)
        row_k = taper(row_cell - place[0:1, :]) * living
        col_k = taper(col_cell - place[1:2, :])
        weight = jnp.concatenate([row_k[i : i + 1, :] * col_k for i in range(WIN_ROWS)], axis=0)
        weight = weight.astype(jnp.bfloat16)
        data = data_ref[pair, 16 * s : 16 * (s + 1)].astype(jnp.float32)
        frame = frame_ref[t % DEPTH, 0, 2 * (a * (tiles // DEPTH) + t // DEPTH) + s]
        scale = [basis_ref[r, frame] for r in range(RANK)]
        across = (((1,), (1,)), ((), ()))
        halves = []
        for half in (data[0:8], data[8:16]):
            values = jnp.concatenate([half * c for c in scale], axis=0).astype(jnp.bfloat16)
            values = jnp.concatenate([values, zero], axis=0)
            halves.append(lax.dot_general(weight, values, across, preferred_element_type=jnp.float32))
        return halves

    def step(a, carry):
        slot_ids = [(t, s) for t in range(tiles) for s in range(slots)]
        sums = [contribution(a, t, s) for t, s in slot_ids]
        for (t, s), halves in zip(slot_ids, sums):
            row = window_ref[a, s, 0, t] + 2
            col = window_ref[a, s, 1, t]
            for i in range(WIN_ROWS):
                for h, half in enumerate(halves):
                    at = (h, row + i, pl.ds(col, WIN_COLS), slice(None))
                    acc_ref[at] += half[i * WIN_COLS : (i + 1) * WIN_COLS]
        return carry

    lax.fori_loop(0, parts, step, 0)


def grid_kernel(window_ref, live_ref, frame_ref, basis_ref, pos_ref, data_ref, _,
                inner_ref, own_ref, up_ref, down_ref, acc_ref):
    grid_slots(window_ref, live_ref, frame_ref, basis_ref, pos_ref, data_ref, acc_ref)

    def fold(row, carry):
        for h in range(2):
            acc_ref[h, row, 0:WIN_COLS, :] += acc_ref[h, row, PLANE:PAD, :]
        return carry

    lax.fori_loop(0, acc_ref.shape[1], fold, 0)

    def put(out_ref, k, row):
        for h in range(2):
            out_ref[k, :, h * LANES : (h + 1) * LANES] = acc_ref[h, row, 0:PLANE, :].astype(out_ref.dtype)

    def put_dense(c, carry):
        for out_ref, first in ((up_ref, 0), (down_ref, TILE_ROWS + 2)):
            for k in range(2):
                pieces = [
                    acc_ref[h, first + k, pl.ds(pl.multiple_of(q * QUARTER + c * WIN_COLS, WIN_COLS), WIN_COLS), :]
                    for q in range(4) for h in range(2)
                ]
                at = pl.ds(pl.multiple_of(c * WIN_COLS, WIN_COLS), WIN_COLS)
                out_ref[k, at, :] = jnp.concatenate(interleave(pieces), axis=1).astype(jnp.bfloat16)
        return carry

    lax.fori_loop(0, QUARTER // WIN_COLS, put_dense, 0)
    for k in range(2):
        put(own_ref, k, 2 + k)
        put(own_ref, 2 + k, TILE_ROWS + k)

    def emit(k, carry):
        put(inner_ref, k, k + 4)
        return carry

    lax.fori_loop(0, TILE_ROWS - 4, emit, 0)


def grid_tile(window, live, frames, basis, pos, data, sums):
    wide = 2 * LANES
    return pl.pallas_call(
        grid_kernel,
        out_shape=[
            jax.ShapeDtypeStruct((TILE_ROWS - 4, PLANE, wide), jnp.bfloat16),
            jax.ShapeDtypeStruct((4, PLANE, wide), jnp.float32),
            jax.ShapeDtypeStruct((2, QUARTER, PLANE), jnp.bfloat16),
            jax.ShapeDtypeStruct((2, QUARTER, PLANE), jnp.bfloat16),
            jax.ShapeDtypeStruct(sums.shape, sums.dtype),
        ],
        in_specs=[SMEM] * 4 + [VMEM] * 3,
        out_specs=[VMEM] * 5,
        input_output_aliases={6: 4},
        compiler_params=pltpu.CompilerParams(vmem_limit_bytes=24 * MB),
        cost_estimate=pl.CostEstimate(flops=6 * 10**9, bytes_accessed=20 * MB, transcendentals=0),
        name="grid_tile",
    )(window, live, frames, basis, pos, data, sums)[:4]


def interleave(pieces):
    lane = lax.broadcasted_iota(jnp.int32, pieces[0].shape, 1)
    p = [pieces[0]] + [pltpu.roll(pieces[k], (HALF * k) % LANES, 1) for k in range(1, 8)]
    return [
        jnp.where(lane < 80, p[0], p[1]),
        jnp.where(lane < 32, p[1], jnp.where(lane < 112, p[2], p[3])),
        jnp.where(lane < 64, p[3], p[4]),
        jnp.where(lane < 16, p[4], jnp.where(lane < 96, p[5], p[6])),
        jnp.where(lane < 48, p[6], p[7]),
    ]


def separate(dense):
    lane = lax.broadcasted_iota(jnp.int32, (dense.shape[0], LANES), 1)
    pieces = []
    for k in range(8):
        tile, start = divmod(HALF * k, LANES)
        piece = dense[:, tile * LANES : (tile + 1) * LANES]
        if start + HALF > LANES:
            piece = jnp.where(lane >= start, piece, dense[:, (tile + 1) * LANES : (tile + 2) * LANES])
        if start:
            piece = pltpu.roll(piece, LANES - start, 1)
        pieces.append(jnp.where(lane < HALF, piece, 0.0))
    return pieces


def mid_kernel(ky_ref, inner_table_ref, edge_table_ref, grid_ref, own_ref, up_ref, down_ref, out_ref,
               send_in, send_ed, recv_in, recv_ed, halo, rot, edge_grid, edge_rot, re_ref, im_ref, edge_kx,
               halo_send, halo_recv, send_sem_in, recv_sem_in, send_sem_ed, recv_sem_ed):
    count = lax.axis_size("tile")
    me = lax.axis_index("tile")
    above = lax.rem(me + count - 1, count)
    below = lax.rem(me + 1, count)
    stages = ky_ref.shape[0]
    inner_rows = TILE_ROWS - 4

    barrier = pltpu.get_barrier_semaphore()

    def greet(k, carry):
        pl.semaphore_signal(
            barrier, inc=1, device_id={"tile": lax.rem(me + k, count)}, device_id_type=pl.DeviceIdType.MESH
        )
        return carry

    lax.fori_loop(1, count, greet, 0)
    pl.semaphore_wait(barrier, count - 1)

    def halo_copy(source, way, peer):
        return pltpu.make_async_remote_copy(
            src_ref=source, dst_ref=halo.at[way], send_sem=halo_send.at[way], recv_sem=halo_recv.at[way],
            device_id={"tile": peer}, device_id_type=pl.DeviceIdType.MESH,
        )

    to_below = halo_copy(down_ref, 0, below)
    to_above = halo_copy(up_ref, 1, above)
    to_below.start()
    to_above.start()

    def turned(plane):
        return jnp.concatenate([-plane[:, LANES:], plane[:, :LANES]], axis=1)

    def turn(k, carry):
        rot[k] = turned(grid_ref[k])
        return carry

    lax.fori_loop(0, inner_rows, turn, 0)

    def rows_of(b, k, plane_ref, turned_ref):
        out = jnp.dot(ky_ref[b, :, :PLANE], plane_ref[k], preferred_element_type=jnp.float32)
        out += jnp.dot(ky_ref[b, :, PLANE:], turned_ref[k], preferred_element_type=jnp.float32)
        at = pl.ds(pl.multiple_of(k * LANES, LANES), LANES)
        re_ref[at, :] = out[:, :LANES]
        im_ref[at, :] = out[:, LANES:]

    def pieces_of(start, size):
        pieces = []
        for j in range(4):
            at = pl.ds(start + j, size, stride=LANES)
            pieces += [re_ref[at, :], im_ref[at, :]]
        return jnp.concatenate(interleave(pieces), axis=1)

    def send_all(b, send, recv, send_sem, recv_sem):
        recv[b, me] = send[b, me]

        def to_peer(k, carry):
            peer = lax.rem(me + k, count)
            pltpu.make_async_remote_copy(
                src_ref=send.at[b, peer], dst_ref=recv.at[b, me],
                send_sem=send_sem.at[b], recv_sem=recv_sem.at[b],
                device_id={"tile": peer}, device_id_type=pl.DeviceIdType.MESH,
            ).start()
            return carry

        lax.fori_loop(1, count, to_peer, 0)

    def stage(b, carry):
        def inner_row(k, carry):
            rows_of(b, k, grid_ref, rot)
            return carry

        lax.fori_loop(0, inner_rows, inner_row, 0, unroll=4)

        def inner_pack(d, carry):
            halves = [pieces_of(g * 8 * LANES + d * 4, 8) for g in range(2)]
            send_in[b, d] = jnp.concatenate(halves, axis=0).astype(jnp.bfloat16)
            return carry

        lax.fori_loop(0, count, inner_pack, 0, unroll=4)
        send_all(b, send_in, recv_in, send_sem_in, recv_sem_in)

        @pl.when(b == 0)
        def _():
            to_below.wait()
            to_above.wait()

            def add_halo(c, carry):
                for k in range(4):
                    at = pl.ds(pl.multiple_of(c * WIN_COLS, WIN_COLS), WIN_COLS)
                    pieces = separate(halo[k // 2, k % 2, at, :].astype(jnp.float32))
                    for p, piece in enumerate(pieces):
                        cols = pl.ds(pl.multiple_of(p // 2 * QUARTER + c * WIN_COLS, WIN_COLS), WIN_COLS)
                        lanes = slice(p % 2 * LANES, (p % 2 + 1) * LANES)
                        edge_grid[k, cols, lanes] = (own_ref[k, cols, lanes] + piece).astype(jnp.bfloat16)
                return carry

            lax.fori_loop(0, QUARTER // WIN_COLS, add_halo, 0)
            for k in range(4):
                edge_rot[k] = turned(edge_grid[k])

        def edge_row(k, carry):
            rows_of(b, k, edge_grid, edge_rot)
            return carry

        lax.fori_loop(0, 4, edge_row, 0, unroll=4)

        def edge_pack(d, carry):
            send_ed[b, d] = pieces_of(d * 4, 4).astype(jnp.bfloat16)
            return carry

        lax.fori_loop(0, count, edge_pack, 0, unroll=4)
        send_all(b, send_ed, recv_ed, send_sem_ed, recv_sem_ed)
        return carry

    lax.fori_loop(0, stages, stage, 0)

    lane = lax.rem(lax.broadcasted_iota(jnp.int32, (320, PLANE), 1), 2 * HALF)
    real = lane < HALF

    def others(b, ref, send_sem, recv_sem):
        return pltpu.make_async_remote_copy(
            src_ref=ref.at[b, pl.ds(0, count - 1)], dst_ref=ref.at[b, pl.ds(0, count - 1)],
            send_sem=send_sem.at[b], recv_sem=recv_sem.at[b],
            device_id={"tile": below}, device_id_type=pl.DeviceIdType.MESH,
        )

    def finish(b, carry):
        others(b, recv_in, send_sem_in, recv_sem_in).wait_recv()
        others(b, recv_ed, send_sem_ed, recv_sem_ed).wait_recv()

        def lift(s, carry):
            pair = [recv_ed[b, 2 * s + k].astype(jnp.float32) for k in range(2)]
            edge_kx[pl.ds(pl.multiple_of(8 * s, 8), 8), :] = jnp.concatenate(pair, axis=0)
            return carry

        lax.fori_loop(0, count // 2, lift, 0)
        inner = recv_in[b].reshape(count * inner_rows, PLANE)
        edge = edge_kx[...].astype(jnp.bfloat16)
        for h in range(2):
            rows = slice(320 * h, 320 * (h + 1))

            def product(part):
                return jnp.dot(
                    inner_table_ref[part, rows, :], inner, preferred_element_type=jnp.float32
                ) + jnp.dot(edge_table_ref[part, rows, :], edge, preferred_element_type=jnp.float32)

            first = product(0)
            second = product(1)
            ahead = pltpu.roll(second, PLANE - HALF, 1)
            behind = pltpu.roll(second, HALF, 1)
            out = first + jnp.where(real, -ahead, behind)
            at = pl.ds(pl.multiple_of(b * PLANE, PLANE), PLANE)
            out_ref[rows, at] = (out * (1.0 / PLANE)).astype(jnp.bfloat16)
        return carry

    lax.fori_loop(0, stages, finish, 0)

    def sent(b, carry):
        others(b, send_in, send_sem_in, recv_sem_in).wait_send()
        others(b, send_ed, send_sem_ed, recv_sem_ed).wait_send()
        return carry

    lax.fori_loop(0, stages, sent, 0)


def transform_plane(ky_table, inner_table, edge_table, grid, own, up, down):
    stages, count, rows, wide = 5, 32, TILE_ROWS - 4, 2 * LANES
    bf16, f32 = jnp.bfloat16, jnp.float32
    dma = pltpu.SemaphoreType.DMA
    return pl.pallas_call(
        mid_kernel,
        out_shape=jax.ShapeDtypeStruct((PLANE, stages * PLANE), bf16),
        in_specs=[VMEM] * 7,
        out_specs=VMEM,
        scratch_shapes=[
            pltpu.VMEM((stages, count, rows, PLANE), bf16),
            pltpu.VMEM((stages, count, 4, PLANE), bf16),
            pltpu.VMEM((stages, count, rows, PLANE), bf16),
            pltpu.VMEM((stages, count, 4, PLANE), bf16),
            pltpu.VMEM((2, 2, QUARTER, PLANE), bf16),
            pltpu.VMEM((rows, PLANE, wide), bf16),
            pltpu.VMEM((4, PLANE, wide), bf16),
            pltpu.VMEM((4, PLANE, wide), bf16),
            pltpu.VMEM((rows * LANES, LANES), f32),
            pltpu.VMEM((rows * LANES, LANES), f32),
            pltpu.VMEM((4 * count, PLANE), f32),
            dma((2,)), dma((2,)), dma((stages,)), dma((stages,)), dma((stages,)), dma((stages,)),
        ],
        compiler_params=pltpu.CompilerParams(
            vmem_limit_bytes=36 * MB, collective_id=0, has_side_effects=True
        ),
        cost_estimate=pl.CostEstimate(flops=20 * 10**9, bytes_accessed=20 * MB, transcendentals=0),
        name="plane",
    )(ky_table, inner_table, edge_table, grid, own, up, down)


def make_tables():
    idx = np.arange(PLANE)
    phase = (idx[:, None] * idx[None, :] % PLANE).astype(np.float32) * np.float32(2.0 * math.pi / PLANE)
    cos_tab = np.cos(phase).astype(ml_dtypes.bfloat16)
    sin_tab = np.sin(phase).astype(ml_dtypes.bfloat16)
    ky_table = np.concatenate([cos_tab, sin_tab], axis=1)
    ky_table = ky_table.reshape(32, 5, 4, 2 * PLANE).transpose(1, 0, 2, 3).reshape(5, LANES, 2 * PLANE)
    both = np.stack([cos_tab, sin_tab]).reshape(2, PLANE, 32, TILE_ROWS)
    inner_table = both[..., 2:18].reshape(2, PLANE, 512)
    edge_table = np.concatenate([both[..., 0:2], both[..., 18:20]], axis=-1).reshape(2, PLANE, 128)
    return ky_table, inner_table, edge_table


def body(coil_data, frame_of, basis, sample_pos, window_at, live_count):
    parts, tiles, slots, pair, samples = coil_data.shape[2:]
    devices = parts * tiles
    frames = frame_of[0, 0].transpose(0, 2, 1)
    data, frames, table, sums = exchange(frames, basis.T, coil_data.reshape(devices, slots * pair, samples))
    window = window_at[0, 0].transpose(0, 2, 3, 1)
    pos = sample_pos.reshape(devices * slots, 2, samples)
    inner, own, up, down = grid_tile(window, live_count[0, 0], frames, table, pos, data, sums)
    ky_table, inner_table, edge_table = [jnp.asarray(t) for t in make_tables()]
    return transform_plane(ky_table, inner_table, edge_table, inner, own, up, down)[None]


def solution(mesh):
    return jax.shard_map(
        body,
        mesh=mesh,
        in_specs=(
            P("kz", "tile", None, None, None, None, None),
            P("kz", "tile", None, None, None),
            P(),
            P("kz", "tile", None, None, None, None, None),
            P("kz", "tile", None, None, None, None),
            P("kz", "tile", None, None),
        ),
        out_specs=P("kz", None, "tile"),
        check_vma=False,
    )
```

```python
import functools
import math

import jax
import jax.numpy as jnp
from jax import lax
from jax.experimental import pallas as pl
from jax.experimental.pallas import tpu as pltpu
from jax.sharding import PartitionSpec as P
import ml_dtypes
import numpy as np

PLANE = 640
WIN_ROWS = 4
WIN_COLS = 32
TILE_ROWS = 20
PAD = PLANE + WIN_COLS
LANES = 128
HALF = 80
QUARTER = PLANE // 4
RANK = 10
DEPTH = 8
MB = 1024 * 1024


def taper(dist):
    inner = 1.0 - (dist * (1.0 / 1.5)) * (dist * (1.0 / 1.5))
    inner = jnp.maximum(inner, 0.0)
    return inner * inner


SMEM = pl.BlockSpec(memory_space=pltpu.SMEM)
VMEM = pl.BlockSpec(memory_space=pltpu.VMEM)
HBM = pl.BlockSpec(memory_space=pltpu.HBM)


def exchange_kernel(frame_ref, basis_ref, data_ref, data_out, frame_out, basis_out, sums_out, spread, met, total,
                    ready, data_send, data_recv, met_send, met_recv, frame_send, frame_recv, own_sem):
    parts, tiles = lax.axis_size("kz"), lax.axis_size("tile")
    kz, tile = lax.axis_index("kz"), lax.axis_index("tile")
    devices = parts * tiles
    me = kz * tiles + tile
    barrier = pltpu.get_barrier_semaphore()

    def signal(sem, part, spot):
        pl.semaphore_signal(sem, inc=1, device_id=(part, spot), device_id_type=pl.DeviceIdType.MESH)

    def greet_tile(k, carry):
        signal(barrier, kz, lax.rem(tile + k, tiles))
        return carry

    def greet_part(k, carry):
        signal(barrier, lax.rem(kz + k, parts), tile)
        return carry

    def tell_part(k, carry):
        signal(ready, lax.rem(kz + k, parts), tile)
        return carry

    lax.fori_loop(1, tiles, greet_tile, 0)
    lax.fori_loop(1, parts, greet_part, 0)
    pl.semaphore_wait(barrier, tiles + parts - 2)
    lax.fori_loop(1, parts, tell_part, 0)

    def copy_to(part, spot, src, dst, send, recv):
        return pltpu.make_async_remote_copy(
            src_ref=src, dst_ref=dst, send_sem=send, recv_sem=recv,
            device_id=(part, spot), device_id_type=pl.DeviceIdType.MESH,
        )

    def send_data(k, carry):
        part = lax.rem(kz + k // tiles, parts)
        spot = lax.rem(tile + lax.rem(k, tiles), tiles)
        to = part * tiles + spot
        copy_to(part, spot, data_ref.at[to], data_out.at[me], data_send, data_recv).start()
        return carry

    lax.fori_loop(1, tiles, send_data, 0)

    columns = tiles // DEPTH
    groups = parts * columns
    column, level = tile // DEPTH, lax.rem(tile, DEPTH)
    mine = kz * columns + column
    lane = lax.broadcasted_iota(jnp.int32, (1, LANES), 1)

    def place(d, carry):
        first, second = [frame_ref[d // tiles, s, lax.rem(d, tiles)] for s in range(2)]
        spread[d] = jnp.where(lane == 2 * mine, first, jnp.where(lane == 2 * mine + 1, second, 0))
        return carry

    lax.fori_loop(0, devices, place, 0, unroll=8)

    pl.semaphore_wait(ready, parts - 1)

    def send_met(k, carry):
        group = lax.rem(mine + k, groups)
        part, spot = group // columns, lax.rem(group, columns) * DEPTH + level
        levels = pl.ds(group * DEPTH, DEPTH)
        copy_to(part, spot, spread.at[levels], met.at[mine], met_send, met_recv).start()
        return carry

    lax.fori_loop(1, groups, send_met, 0)
    lax.fori_loop(tiles, devices, send_data, 0)
    own = pltpu.make_async_copy(data_ref.at[me], data_out.at[me], own_sem)
    own.start()
    met[mine] = spread[pl.ds(mine * DEPTH, DEPTH)]
    basis_out[...] = basis_ref[...].astype(jnp.float32)
    others = pl.ds(0, groups - 1)
    rows = pl.ds(0, (groups - 1) * DEPTH)
    copy_to(kz, lax.rem(tile + 1, tiles), spread.at[rows], spread.at[rows], met_send, met_recv).wait_send()
    copy_to(kz, lax.rem(tile + 1, tiles), met.at[others], met.at[others], met_send, met_recv).wait_recv()

    def add(g, carry):
        return carry + met[g]

    total[...] = lax.fori_loop(0, groups, add, jnp.zeros(total.shape, jnp.int32))

    def send_frames(k, carry):
        to = lax.rem(level + k, DEPTH)
        copy_to(kz, column * DEPTH + to, total.at[to], frame_out.at[level], frame_send, frame_recv).start()
        return carry

    lax.fori_loop(1, DEPTH, send_frames, 0)
    frame_out[level] = total[level]

    def clear(k, carry):
        for h in range(2):
            sums_out[h, k] = jnp.zeros(sums_out.shape[2:], jnp.float32)
        return carry

    lax.fori_loop(0, sums_out.shape[1], clear, 0)
    own.wait()
    others = pl.ds(0, devices - 1)
    levels = pl.ds(0, DEPTH - 1)
    beside = (kz, lax.rem(tile + 1, tiles))
    for every in (
        copy_to(*beside, data_ref.at[others], data_out.at[others], data_send, data_recv),
        copy_to(*beside, total.at[levels], frame_out.at[levels], frame_send, frame_recv),
    ):
        every.wait_send()
        every.wait_recv()


def exchange(frames, basis, data):
    dma = pltpu.SemaphoreType.DMA
    devices = data.shape[0]
    groups = devices // DEPTH
    return pl.pallas_call(
        exchange_kernel,
        out_shape=[
            jax.ShapeDtypeStruct(data.shape, data.dtype),
            jax.ShapeDtypeStruct((DEPTH, 1, LANES), jnp.int32),
            jax.ShapeDtypeStruct(basis.shape, jnp.float32),
            jax.ShapeDtypeStruct((2, TILE_ROWS + 4, PAD, LANES), jnp.float32),
        ],
        in_specs=[SMEM, VMEM, HBM],
        out_specs=[VMEM] * 4,
        scratch_shapes=[
            pltpu.VMEM((devices, 1, LANES), jnp.int32),
            pltpu.VMEM((groups, DEPTH, 1, LANES), jnp.int32),
            pltpu.VMEM((DEPTH, 1, LANES), jnp.int32),
            pltpu.SemaphoreType.REGULAR,
        ] + [dma] * 7,
        compiler_params=pltpu.CompilerParams(collective_id=1, has_side_effects=True, vmem_limit_bytes=8 * MB),
        cost_estimate=pl.CostEstimate(flops=6 * 10**10, bytes_accessed=4 * MB, transcendentals=0),
        name="exchange",
    )(frames, basis, data)


def grid_slots(window_ref, live_ref, frame_ref, basis_ref, pos_ref, data_ref, acc_ref):
    parts, slots, _, tiles = window_ref.shape
    row_cell = lax.broadcasted_iota(jnp.int32, (8, LANES), 0).astype(jnp.float32)
    col_cell = lax.broadcasted_iota(jnp.int32, (WIN_COLS, LANES), 0).astype(jnp.float32)
    zero = jnp.zeros((LANES - HALF, LANES), jnp.bfloat16)

    def contribution(a, t, s):
        pair = a * tiles + t
        place = pos_ref[pair * slots + s]
        living = (s < live_ref[a, t]).astype(jnp.float32)
        row_k = taper(row_cell - place[0:1, :]) * living
        col_k = taper(col_cell - place[1:2, :])
        weight = jnp.concatenate([row_k[i : i + 1, :] * col_k for i in range(WIN_ROWS)], axis=0)
        weight = weight.astype(jnp.bfloat16)
        data = data_ref[pair, 16 * s : 16 * (s + 1)].astype(jnp.float32)
        frame = frame_ref[t % DEPTH, 0, 2 * (a * (tiles // DEPTH) + t // DEPTH) + s]
        scale = [basis_ref[r, frame] for r in range(RANK)]
        across = (((1,), (1,)), ((), ()))
        halves = []
        for half in (data[0:8], data[8:16]):
            values = jnp.concatenate([half * c for c in scale], axis=0).astype(jnp.bfloat16)
            values = jnp.concatenate([values, zero], axis=0)
            halves.append(lax.dot_general(weight, values, across, preferred_element_type=jnp.float32))
        return halves

    def step(a, carry):
        slot_ids = [(t, s) for t in range(tiles) for s in range(slots)]
        sums = [contribution(a, t, s) for t, s in slot_ids]
        for (t, s), halves in zip(slot_ids, sums):
            row = window_ref[a, s, 0, t] + 2
            col = window_ref[a, s, 1, t]
            for i in range(WIN_ROWS):
                for h, half in enumerate(halves):
                    at = (h, row + i, pl.ds(col, WIN_COLS), slice(None))
                    acc_ref[at] += half[i * WIN_COLS : (i + 1) * WIN_COLS]
        return carry

    lax.fori_loop(0, parts, step, 0)


def grid_kernel(window_ref, live_ref, frame_ref, basis_ref, pos_ref, data_ref, _,
                inner_ref, own_ref, up_ref, down_ref, acc_ref):
    grid_slots(window_ref, live_ref, frame_ref, basis_ref, pos_ref, data_ref, acc_ref)

    def fold(row, carry):
        for h in range(2):
            acc_ref[h, row, 0:WIN_COLS, :] += acc_ref[h, row, PLANE:PAD, :]
        return carry

    lax.fori_loop(0, acc_ref.shape[1], fold, 0)

    def put(out_ref, k, row):
        for h in range(2):
            out_ref[k, :, h * LANES : (h + 1) * LANES] = acc_ref[h, row, 0:PLANE, :].astype(out_ref.dtype)

    def put_dense(c, carry):
        for out_ref, first in ((up_ref, 0), (down_ref, TILE_ROWS + 2)):
            for k in range(2):
                pieces = [
                    acc_ref[h, first + k, pl.ds(pl.multiple_of(q * QUARTER + c * WIN_COLS, WIN_COLS), WIN_COLS), :]
                    for q in range(4) for h in range(2)
                ]
                at = pl.ds(pl.multiple_of(c * WIN_COLS, WIN_COLS), WIN_COLS)
                out_ref[k, at, :] = jnp.concatenate(interleave(pieces), axis=1).astype(jnp.bfloat16)
        return carry

    lax.fori_loop(0, QUARTER // WIN_COLS, put_dense, 0)
    for k in range(2):
        put(own_ref, k, 2 + k)
        put(own_ref, 2 + k, TILE_ROWS + k)

    def emit(k, carry):
        put(inner_ref, k, k + 4)
        return carry

    lax.fori_loop(0, TILE_ROWS - 4, emit, 0)


def grid_tile(window, live, frames, basis, pos, data, sums):
    wide = 2 * LANES
    return pl.pallas_call(
        grid_kernel,
        out_shape=[
            jax.ShapeDtypeStruct((TILE_ROWS - 4, PLANE, wide), jnp.bfloat16),
            jax.ShapeDtypeStruct((4, PLANE, wide), jnp.float32),
            jax.ShapeDtypeStruct((2, QUARTER, PLANE), jnp.bfloat16),
            jax.ShapeDtypeStruct((2, QUARTER, PLANE), jnp.bfloat16),
            jax.ShapeDtypeStruct(sums.shape, sums.dtype),
        ],
        in_specs=[SMEM] * 4 + [VMEM] * 3,
        out_specs=[VMEM] * 5,
        input_output_aliases={6: 4},
        compiler_params=pltpu.CompilerParams(vmem_limit_bytes=24 * MB),
        cost_estimate=pl.CostEstimate(flops=6 * 10**9, bytes_accessed=20 * MB, transcendentals=0),
        name="grid_tile",
    )(window, live, frames, basis, pos, data, sums)[:4]


def interleave(pieces):
    lane = lax.broadcasted_iota(jnp.int32, pieces[0].shape, 1)
    p = [pieces[0]] + [pltpu.roll(pieces[k], (HALF * k) % LANES, 1) for k in range(1, 8)]
    return [
        jnp.where(lane < 80, p[0], p[1]),
        jnp.where(lane < 32, p[1], jnp.where(lane < 112, p[2], p[3])),
        jnp.where(lane < 64, p[3], p[4]),
        jnp.where(lane < 16, p[4], jnp.where(lane < 96, p[5], p[6])),
        jnp.where(lane < 48, p[6], p[7]),
    ]


def separate(dense):
    lane = lax.broadcasted_iota(jnp.int32, (dense.shape[0], LANES), 1)
    pieces = []
    for k in range(8):
        tile, start = divmod(HALF * k, LANES)
        piece = dense[:, tile * LANES : (tile + 1) * LANES]
        if start + HALF > LANES:
            piece = jnp.where(lane >= start, piece, dense[:, (tile + 1) * LANES : (tile + 2) * LANES])
        if start:
            piece = pltpu.roll(piece, LANES - start, 1)
        pieces.append(jnp.where(lane < HALF, piece, 0.0))
    return pieces


def joined(first, second):
    lane = lax.rem(lax.broadcasted_iota(jnp.int32, first.shape, 1), 2 * HALF)
    ahead = pltpu.roll(second, PLANE - HALF, 1)
    behind = pltpu.roll(second, HALF, 1)
    out = first + jnp.where(lane < HALF, -ahead, behind)
    return (out * (1.0 / PLANE)).astype(jnp.bfloat16)


def last_stage(edge_table_ref, before_ref, sums_ref, edge_ref, out_ref, block, sems):
    done = before_ref.shape[1]
    early = pltpu.make_async_copy(before_ref, out_ref.at[:, pl.ds(0, done)], sems.at[0])
    early.start()
    for h in range(2):
        rows = slice(320 * h, 320 * (h + 1))
        first, second = [
            sums_ref[part, rows, :]
            + jnp.dot(edge_table_ref[part, rows, :], edge_ref[...], preferred_element_type=jnp.float32)
            for part in range(2)
        ]
        block[rows, :] = joined(first, second)
    late = pltpu.make_async_copy(block, out_ref.at[:, pl.ds(done, PLANE)], sems.at[1])
    late.start()
    early.wait()
    late.wait()


def mid_kernel(ky_ref, inner_table_ref, edge_table_ref, grid_ref, own_ref, up_ref, down_ref, out_ref, last_ref, edge_ref,
               send_in, send_ed, recv_in, recv_ed, halo, rot, edge_grid, edge_rot, re_ref, im_ref, edge_kx,
               halo_send, halo_recv, send_sem_in, recv_sem_in, send_sem_ed, recv_sem_ed):
    count = lax.axis_size("tile")
    me = lax.axis_index("tile")
    above = lax.rem(me + count - 1, count)
    below = lax.rem(me + 1, count)
    stages = ky_ref.shape[0]
    inner_rows = TILE_ROWS - 4

    barrier = pltpu.get_barrier_semaphore()

    def greet(k, carry):
        pl.semaphore_signal(
            barrier, inc=1, device_id={"tile": lax.rem(me + k, count)}, device_id_type=pl.DeviceIdType.MESH
        )
        return carry

    lax.fori_loop(1, count, greet, 0)
    pl.semaphore_wait(barrier, count - 1)

    def halo_copy(source, way, peer):
        return pltpu.make_async_remote_copy(
            src_ref=source, dst_ref=halo.at[way], send_sem=halo_send.at[way], recv_sem=halo_recv.at[way],
            device_id={"tile": peer}, device_id_type=pl.DeviceIdType.MESH,
        )

    to_below = halo_copy(down_ref, 0, below)
    to_above = halo_copy(up_ref, 1, above)
    to_below.start()
    to_above.start()

    def turned(plane):
        return jnp.concatenate([-plane[:, LANES:], plane[:, :LANES]], axis=1)

    def turn(k, carry):
        rot[k] = turned(grid_ref[k])
        return carry

    lax.fori_loop(0, inner_rows, turn, 0)

    def rows_of(b, k, plane_ref, turned_ref):
        out = jnp.dot(ky_ref[b, :, :PLANE], plane_ref[k], preferred_element_type=jnp.float32)
        out += jnp.dot(ky_ref[b, :, PLANE:], turned_ref[k], preferred_element_type=jnp.float32)
        at = pl.ds(pl.multiple_of(k * LANES, LANES), LANES)
        re_ref[at, :] = out[:, :LANES]
        im_ref[at, :] = out[:, LANES:]

    def pieces_of(start, size):
        pieces = []
        for j in range(4):
            at = pl.ds(start + j, size, stride=LANES)
            pieces += [re_ref[at, :], im_ref[at, :]]
        return jnp.concatenate(interleave(pieces), axis=1)

    def send_all(b, send, recv, send_sem, recv_sem):
        recv[b, me] = send[b, me]

        def to_peer(k, carry):
            peer = lax.rem(me + k, count)
            pltpu.make_async_remote_copy(
                src_ref=send.at[b, peer], dst_ref=recv.at[b, me],
                send_sem=send_sem.at[b], recv_sem=recv_sem.at[b],
                device_id={"tile": peer}, device_id_type=pl.DeviceIdType.MESH,
            ).start()
            return carry

        lax.fori_loop(1, count, to_peer, 0)

    def stage(b, carry):
        def inner_row(k, carry):
            rows_of(b, k, grid_ref, rot)
            return carry

        lax.fori_loop(0, inner_rows, inner_row, 0, unroll=4)

        def inner_pack(d, carry):
            halves = [pieces_of(g * 8 * LANES + d * 4, 8) for g in range(2)]
            send_in[b, d] = jnp.concatenate(halves, axis=0).astype(jnp.bfloat16)
            return carry

        lax.fori_loop(0, count, inner_pack, 0, unroll=4)
        send_all(b, send_in, recv_in, send_sem_in, recv_sem_in)

        @pl.when(b == 0)
        def _():
            to_below.wait()
            to_above.wait()

            def add_halo(c, carry):
                for k in range(4):
                    at = pl.ds(pl.multiple_of(c * WIN_COLS, WIN_COLS), WIN_COLS)
                    pieces = separate(halo[k // 2, k % 2, at, :].astype(jnp.float32))
                    for p, piece in enumerate(pieces):
                        cols = pl.ds(pl.multiple_of(p // 2 * QUARTER + c * WIN_COLS, WIN_COLS), WIN_COLS)
                        lanes = slice(p % 2 * LANES, (p % 2 + 1) * LANES)
                        edge_grid[k, cols, lanes] = (own_ref[k, cols, lanes] + piece).astype(jnp.bfloat16)
                return carry

            lax.fori_loop(0, QUARTER // WIN_COLS, add_halo, 0)
            for k in range(4):
                edge_rot[k] = turned(edge_grid[k])

        def edge_row(k, carry):
            rows_of(b, k, edge_grid, edge_rot)
            return carry

        lax.fori_loop(0, 4, edge_row, 0, unroll=4)

        def edge_pack(d, carry):
            send_ed[b, d] = pieces_of(d * 4, 4).astype(jnp.bfloat16)
            return carry

        lax.fori_loop(0, count, edge_pack, 0, unroll=4)
        send_all(b, send_ed, recv_ed, send_sem_ed, recv_sem_ed)
        return carry

    lax.fori_loop(0, stages, stage, 0)

    def others(b, ref, send_sem, recv_sem):
        return pltpu.make_async_remote_copy(
            src_ref=ref.at[b, pl.ds(0, count - 1)], dst_ref=ref.at[b, pl.ds(0, count - 1)],
            send_sem=send_sem.at[b], recv_sem=recv_sem.at[b],
            device_id={"tile": below}, device_id_type=pl.DeviceIdType.MESH,
        )

    def lift_edges(b):
        def lift(s, carry):
            pair = [recv_ed[b, 2 * s + k].astype(jnp.float32) for k in range(2)]
            edge_kx[pl.ds(pl.multiple_of(8 * s, 8), 8), :] = jnp.concatenate(pair, axis=0)
            return carry

        lax.fori_loop(0, count // 2, lift, 0)
        return edge_kx[...].astype(jnp.bfloat16)

    def finish(b, carry):
        others(b, recv_in, send_sem_in, recv_sem_in).wait_recv()
        others(b, recv_ed, send_sem_ed, recv_sem_ed).wait_recv()
        inner = recv_in[b].reshape(count * inner_rows, PLANE)
        edge = lift_edges(b)
        for h in range(2):
            rows = slice(320 * h, 320 * (h + 1))
            first, second = [
                jnp.dot(inner_table_ref[part, rows, :], inner, preferred_element_type=jnp.float32)
                + jnp.dot(edge_table_ref[part, rows, :], edge, preferred_element_type=jnp.float32)
                for part in range(2)
            ]
            at = pl.ds(pl.multiple_of(b * PLANE, PLANE), PLANE)
            out_ref[rows, at] = joined(first, second)
        return carry

    last = stages - 1
    lax.fori_loop(0, last, finish, 0)
    others(last, recv_in, send_sem_in, recv_sem_in).wait_recv()
    inner = recv_in[last].reshape(count * inner_rows, PLANE)
    for part in range(2):
        for h in range(2):
            rows = slice(320 * h, 320 * (h + 1))
            last_ref[part, rows, :] = jnp.dot(
                inner_table_ref[part, rows, :], inner, preferred_element_type=jnp.float32
            )
    others(last, recv_ed, send_sem_ed, recv_sem_ed).wait_recv()
    edge_ref[...] = lift_edges(last)

    def sent(b, carry):
        others(b, send_in, send_sem_in, recv_sem_in).wait_send()
        others(b, send_ed, send_sem_ed, recv_sem_ed).wait_send()
        return carry

    lax.fori_loop(0, stages, sent, 0)


def transform_plane(ky_table, inner_table, edge_table, grid, own, up, down):
    stages, count, rows, wide = 5, 32, TILE_ROWS - 4, 2 * LANES
    bf16, f32 = jnp.bfloat16, jnp.float32
    dma = pltpu.SemaphoreType.DMA
    parts = pl.pallas_call(
        mid_kernel,
        out_shape=[
            jax.ShapeDtypeStruct((PLANE, (stages - 1) * PLANE), bf16),
            jax.ShapeDtypeStruct((2, PLANE, PLANE), f32),
            jax.ShapeDtypeStruct((4 * count, PLANE), bf16),
        ],
        in_specs=[VMEM] * 7,
        out_specs=[VMEM] * 3,
        scratch_shapes=[
            pltpu.VMEM((stages, count, rows, PLANE), bf16),
            pltpu.VMEM((stages, count, 4, PLANE), bf16),
            pltpu.VMEM((stages, count, rows, PLANE), bf16),
            pltpu.VMEM((stages, count, 4, PLANE), bf16),
            pltpu.VMEM((2, 2, QUARTER, PLANE), bf16),
            pltpu.VMEM((rows, PLANE, wide), bf16),
            pltpu.VMEM((4, PLANE, wide), bf16),
            pltpu.VMEM((4, PLANE, wide), bf16),
            pltpu.VMEM((rows * LANES, LANES), f32),
            pltpu.VMEM((rows * LANES, LANES), f32),
            pltpu.VMEM((4 * count, PLANE), f32),
            dma((2,)), dma((2,)), dma((stages,)), dma((stages,)), dma((stages,)), dma((stages,)),
        ],
        compiler_params=pltpu.CompilerParams(
            vmem_limit_bytes=32 * MB, collective_id=0, has_side_effects=True
        ),
        cost_estimate=pl.CostEstimate(flops=20 * 10**9, bytes_accessed=20 * MB, transcendentals=0),
        name="plane",
    )(ky_table, inner_table, edge_table, grid, own, up, down)
    return pl.pallas_call(
        last_stage,
        out_shape=jax.ShapeDtypeStruct((PLANE, stages * PLANE), bf16),
        in_specs=[VMEM] * 4,
        out_specs=HBM,
        scratch_shapes=[pltpu.VMEM((PLANE, PLANE), bf16), dma((2,))],
        compiler_params=pltpu.CompilerParams(vmem_limit_bytes=16 * MB),
        cost_estimate=pl.CostEstimate(flops=5 * 10**8, bytes_accessed=8 * MB, transcendentals=0),
        name="last_stage",
    )(edge_table, *parts)


def make_tables():
    idx = np.arange(PLANE)
    phase = (idx[:, None] * idx[None, :] % PLANE).astype(np.float32) * np.float32(2.0 * math.pi / PLANE)
    cos_tab = np.cos(phase).astype(ml_dtypes.bfloat16)
    sin_tab = np.sin(phase).astype(ml_dtypes.bfloat16)
    ky_table = np.concatenate([cos_tab, sin_tab], axis=1)
    ky_table = ky_table.reshape(32, 5, 4, 2 * PLANE).transpose(1, 0, 2, 3).reshape(5, LANES, 2 * PLANE)
    both = np.stack([cos_tab, sin_tab]).reshape(2, PLANE, 32, TILE_ROWS)
    inner_table = both[..., 2:18].reshape(2, PLANE, 512)
    edge_table = np.concatenate([both[..., 0:2], both[..., 18:20]], axis=-1).reshape(2, PLANE, 128)
    return ky_table, inner_table, edge_table


def body(coil_data, frame_of, basis, sample_pos, window_at, live_count):
    parts, tiles, slots, pair, samples = coil_data.shape[2:]
    devices = parts * tiles
    frames = frame_of[0, 0].transpose(0, 2, 1)
    data, frames, table, sums = exchange(frames, basis.T, coil_data.reshape(devices, slots * pair, samples))
    window = window_at[0, 0].transpose(0, 2, 3, 1)
    pos = sample_pos.reshape(devices * slots, 2, samples)
    inner, own, up, down = grid_tile(window, live_count[0, 0], frames, table, pos, data, sums)
    ky_table, inner_table, edge_table = [jnp.asarray(t) for t in make_tables()]
    return transform_plane(ky_table, inner_table, edge_table, inner, own, up, down)[None]


def solution(mesh):
    return jax.shard_map(
        body,
        mesh=mesh,
        in_specs=(
            P("kz", "tile", None, None, None, None, None),
            P("kz", "tile", None, None, None),
            P(),
            P("kz", "tile", None, None, None, None, None),
            P("kz", "tile", None, None, None, None),
            P("kz", "tile", None, None),
        ),
        out_specs=P("kz", None, "tile"),
        check_vma=False,
    )
```
